32 devices in a mesh: dp: 8 (over z, y), tensor: 4 (over x, core).
Axes of the slice: x: 2, y: 2, z: 4, core: 2. Of those that a mesh axis runs over, the one named last changes fastest.
Arguments:
- output_gradient: bfloat16 [3072, 8192], P(('dp', 'tensor')), may hold values from -6 to 6
- attention_output: bfloat16 [3072, 8192], P('dp', 'tensor'), may hold values from -0.29882812 to 0.29882812
- frozen_projection: bfloat16 [8192, 8192], P('tensor', 'dp'), may hold values from -0.0625 to 0.0625
- domain_down_map: bfloat16 [4, 32, 8192], P(None, None, 'tensor'), may hold values from -0.29882812 to 0.29882812
- domain_up_map: bfloat16 [4, 32, 8192], P(None, None, 'tensor'), may hold values from -0.0625 to 0.0625
- common_down_map: bfloat16 [16, 8192], P(None, 'tensor'), may hold values from -0.29882812 to 0.29882812
- common_up_map: bfloat16 [16, 8192], P(None, 'tensor'), may hold values from -0.0625 to 0.0625
- live_token_count: int32 [8], P('dp'), may hold values from 128 to 384, as said below
- series_domain: int32 [8], replicated, may hold values from 0 to 3, as said below
Outputs:
- grad_input: bfloat16 [3072, 8192], P('dp', 'tensor')
- domain_down_gradient: float32 [4, 32, 8192], P(None, None, 'tensor')
- domain_up_gradient: float32 [4, 32, 8192], P(None, None, 'tensor')
- common_down_gradient: float32 [16, 8192], P(None, 'tensor')
- common_up_gradient: float32 [16, 8192], P(None, 'tensor')
The draws below stay inside these ranges and needn't reach their ends.
Inputs may be any that keep to these rules, and one draw needn't show every extreme that they name: `live_token_count`: a multiple of 128; some series has exactly 384. `series_domain`: every domain is named by at least one series.
All inputs are finite; a program needn't handle non-finite values.
Results may differ from the reference program's by a relative error of at most 0.0035.
Values may be sent and summed in bfloat16 or wider, within the bound.
A program may use at most 128 MiB of HBM per device.

```python
import jax
import jax.numpy as jnp
from jax import lax

MODEL_WIDTH = 8192
QUERY_HEAD_WIDTH = 8192
ADAPTER_RANK = 32
SRANK = 16
DOMAIN_COUNT = 4
BLOCK = 128
SERIES_TOKENS = 384
ALL_TOK = 3072
N_DP = 8


def draw_live_token_count(key, part):
    blocks_all = SERIES_TOKENS // BLOCK
    rank_ids = jnp.arange(N_DP, dtype=jnp.int32)
    extra_blocks = jax.random.randint(jax.random.fold_in(key, 11), (N_DP,), 0, 2)
    blocks = jnp.minimum(blocks_all, 1 + rank_ids * blocks_all // N_DP + extra_blocks)
    return (blocks * BLOCK).astype(jnp.int32)


def draw_series_domain(key, part):
    shuffled = jax.random.permutation(jax.random.fold_in(key, 21), N_DP)
    first_draw = jax.random.randint(jax.random.fold_in(key, 22), (N_DP,), 0, DOMAIN_COUNT)
    second_draw = jax.random.randint(jax.random.fold_in(key, 23), (N_DP,), 0, DOMAIN_COUNT)
    skewed = jnp.minimum(first_draw, second_draw).astype(jnp.int32)
    return skewed.at[shuffled[:DOMAIN_COUNT]].set(jnp.arange(DOMAIN_COUNT, dtype=jnp.int32)).astype(jnp.int32)


def block_levels(own_key, extent, shards, least, largest):
    loudness, own = 1.0, jax.random.fold_in(own_key, 6)
    for axis_at, shards_of in shards:
        draws = jnp.exp(jax.random.uniform(jax.random.fold_in(own, axis_at), (shards_of,), jnp.float32, least / len(shards), largest / len(shards)))
        loudness = loudness * jnp.repeat(draws, extent[axis_at] // shards_of).reshape([-1 if axis == axis_at else 1 for axis in range(len(extent))])
    return loudness


def gaussian(rng, extent, deviation, limit, split=(), kind=jnp.bfloat16):
    result = jax.random.normal(rng, extent, jnp.float32) * deviation
    if len(split) > 0:
        result = block_levels(rng, extent, split, -0.22, 0.18) * result
    return jnp.clip(result, min=-limit, max=limit).astype(kind)


def setup_inputs(seed: int = 0) -> dict:
    splits = jax.random.split(jax.random.key(seed), 10)
    output_gradient = gaussian(splits[0], (ALL_TOK, MODEL_WIDTH), 1.0, 6.0, ((0, 32),))
    attention_output = gaussian(splits[1], (ALL_TOK, QUERY_HEAD_WIDTH), 0.05, 0.29882812, ((0, 8), (1, 4)))
    frozen_projection = gaussian(splits[2], (QUERY_HEAD_WIDTH, MODEL_WIDTH), MODEL_WIDTH ** -0.5, 0.0625, ((0, 4), (1, 8)))
    domain_down_map = gaussian(splits[3], (DOMAIN_COUNT, ADAPTER_RANK, QUERY_HEAD_WIDTH), 0.05, 0.29882812, ((2, 4),))
    domain_up_map = gaussian(splits[4], (DOMAIN_COUNT, ADAPTER_RANK, MODEL_WIDTH), MODEL_WIDTH ** -0.5, 0.0625, ((2, 4),))
    common_down_map = gaussian(splits[5], (SRANK, QUERY_HEAD_WIDTH), 0.05, 0.29882812, ((1, 4),))
    common_up_map = gaussian(splits[6], (SRANK, MODEL_WIDTH), MODEL_WIDTH ** -0.5, 0.0625, ((1, 4),))
    live_token_count = draw_live_token_count(jax.random.fold_in(splits[9], 71), 0)
    series_domain = draw_series_domain(jax.random.fold_in(splits[9], 71), 0)
    return {"output_gradient": output_gradient, "attention_output": attention_output, "frozen_projection": frozen_projection, "domain_down_map": domain_down_map, "domain_up_map": domain_up_map, "common_down_map": common_down_map, "common_up_map": common_up_map, "live_token_count": live_token_count, "series_domain": series_domain}


adapter_scale = 2.0
shared_scale = 2.0


def reference(output_gradient, attention_output, frozen_projection, domain_down_map, domain_up_map, common_down_map, common_up_map, live_token_count, series_domain):
    grad_seq = output_gradient.reshape(N_DP, SERIES_TOKENS, MODEL_WIDTH)
    act_seq = attention_output.reshape(N_DP, SERIES_TOKENS, QUERY_HEAD_WIDTH)
    positions = lax.iota(jnp.int32, SERIES_TOKENS)
    live_rows = positions[None, :] < live_token_count[:, None]
    masked = jnp.where(live_rows[:, :, None], grad_seq, jnp.zeros_like(grad_seq))

    def per_rank(operands):
        gradient_rows, activation_rows, domain_label = operands
        local_down_map = lax.dynamic_index_in_dim(domain_down_map, domain_label, 0, keepdims=False)
        local_up_map = lax.dynamic_index_in_dim(domain_up_map, domain_label, 0, keepdims=False)
        reduced_activation = jnp.dot(activation_rows, local_down_map.T, preferred_element_type=jnp.float32).astype(jnp.bfloat16)
        low_shared = jnp.dot(activation_rows, common_down_map.T, preferred_element_type=jnp.float32).astype(jnp.bfloat16)
        domain_backward = jnp.dot(gradient_rows, local_up_map.T, preferred_element_type=jnp.float32).astype(jnp.bfloat16)
        back_shared = jnp.dot(gradient_rows, common_up_map.T, preferred_element_type=jnp.float32).astype(jnp.bfloat16)
        input_gradient = jnp.dot(gradient_rows, frozen_projection.T, preferred_element_type=jnp.float32)
        input_gradient = input_gradient + adapter_scale * jnp.dot(domain_backward, local_down_map, preferred_element_type=jnp.float32)
        input_gradient = input_gradient + shared_scale * jnp.dot(back_shared, common_down_map, preferred_element_type=jnp.float32)
        down_gradient = adapter_scale * jnp.dot(domain_backward.T, activation_rows, preferred_element_type=jnp.float32)
        up_gradient = adapter_scale * jnp.dot(reduced_activation.T, gradient_rows, preferred_element_type=jnp.float32)
        grad_sdown = shared_scale * jnp.dot(back_shared.T, activation_rows, preferred_element_type=jnp.float32)
        grad_sup = shared_scale * jnp.dot(low_shared.T, gradient_rows, preferred_element_type=jnp.float32)
        return input_gradient.astype(jnp.bfloat16), down_gradient, up_gradient, grad_sdown, grad_sup

    input_gradient, down_gradient, up_gradient, grad_sdown, grad_sup = lax.map(per_rank, (masked, act_seq, series_domain))
    domain_picker = (series_domain[:, None] == lax.iota(jnp.int32, DOMAIN_COUNT)[None, :]).astype(jnp.float32)
    domain_down_gradient = jnp.tensordot(domain_picker, down_gradient, axes=(0, 0), precision=lax.Precision.HIGHEST)
    domain_up_gradient = jnp.tensordot(domain_picker, up_gradient, axes=(0, 0), precision=lax.Precision.HIGHEST)
    common_down_gradient = jnp.sum(grad_sdown, axis=0)
    common_up_gradient = jnp.sum(grad_sup, axis=0)
    return (input_gradient.reshape(N_DP * SERIES_TOKENS, QUERY_HEAD_WIDTH), domain_down_gradient, domain_up_gradient, common_down_gradient, common_up_gradient)
```

```python
import functools

import jax
import jax.numpy as jnp
from jax import lax
from jax.experimental import pallas as pl
from jax.experimental.pallas import tpu as pltpu
from jax.sharding import PartitionSpec as P

adapter_scale = 2.0
shared_scale = 2.0
contract_dims = (((1,), (1,)), ((), ()))
outer_dims = (((0,), (0,)), ((), ()))


def on_device(
    output_gradient,
    attention_output,
    frozen_projection,
    domain_down_map,
    domain_up_map,
    common_down_map,
    common_up_map,
    live_token_count,
    series_domain,
):
    rows_local = output_gradient.shape[0]
    tensor_index = lax.axis_index("tensor")
    rank_index = lax.axis_index("dp")
    domain_number = lax.dynamic_index_in_dim(series_domain, rank_index, 0, keepdims=False)
    local_down_map = lax.dynamic_index_in_dim(domain_down_map, domain_number, 0, keepdims=False)
    local_up_map = lax.dynamic_index_in_dim(domain_up_map, domain_number, 0, keepdims=False)
    positions = tensor_index * rows_local + lax.iota(jnp.int32, rows_local)
    live_rows = (positions < live_token_count[0])[:, None]
    masked = jnp.where(live_rows, output_gradient, jnp.zeros_like(output_gradient))
    down_part = lax.dot_general(
        attention_output, local_down_map, contract_dims, preferred_element_type=jnp.float32
    )
    shared_part = lax.dot_general(
        attention_output, common_down_map, contract_dims, preferred_element_type=jnp.float32
    )
    down_total, shared_total = lax.psum((down_part, shared_part), "tensor")
    reduced_activation = down_total.astype(jnp.bfloat16)
    low_shared = shared_total.astype(jnp.bfloat16)
    gathered = lax.all_gather(masked, "tensor", axis=0, tiled=True)
    column_width = local_up_map.shape[1]
    my_columns = lax.dynamic_slice_in_dim(gathered, tensor_index * column_width, column_width, 1)
    dom_partial = lax.dot_general(
        my_columns, local_up_map, contract_dims, preferred_element_type=jnp.float32
    )
    shared_partial = lax.dot_general(
        my_columns, common_up_map, contract_dims, preferred_element_type=jnp.float32
    )
    dom_total, shared_back_total = lax.psum((dom_partial, shared_partial), "tensor")
    domain_backward = dom_total.astype(jnp.bfloat16)
    back_shared = shared_back_total.astype(jnp.bfloat16)
    local_down_gradient = adapter_scale * lax.dot_general(
        domain_backward, attention_output, outer_dims, preferred_element_type=jnp.float32
    )
    local_up_gradient = adapter_scale * lax.dot_general(
        reduced_activation, my_columns, outer_dims, preferred_element_type=jnp.float32
    )
    grad_sdown = shared_scale * lax.dot_general(
        back_shared, attention_output, outer_dims, preferred_element_type=jnp.float32
    )
    grad_sup = shared_scale * lax.dot_general(
        low_shared, my_columns, outer_dims, preferred_element_type=jnp.float32
    )
    domain_picker = (lax.iota(jnp.int32, domain_down_map.shape[0]) == domain_number).astype(
        jnp.float32
    )[:, None, None]
    frozen_total = lax.dot_general(
        gathered,
        lax.all_gather(frozen_projection, "dp", axis=1, tiled=True),
        contract_dims,
        preferred_element_type=jnp.float32,
    )
    summed = lax.psum(
        (
            domain_picker * local_down_gradient[None],
            domain_picker * local_up_gradient[None],
            grad_sdown,
            grad_sup,
        ),
        "dp",
    )
    adapter_contribution = adapter_scale * jnp.dot(
        domain_backward, local_down_map, preferred_element_type=jnp.float32
    )
    adapter_contribution = adapter_contribution + shared_scale * jnp.dot(
        back_shared, common_down_map, preferred_element_type=jnp.float32
    )
    grad_input = (frozen_total + adapter_contribution).astype(jnp.bfloat16)
    return (grad_input, summed[0], summed[1], summed[2], summed[3])

MESH = pl.DeviceIdType.MESH
CHUNK = 256


def nt_dot(left, right):
    return lax.dot_general(left, right, contract_dims, preferred_element_type=jnp.float32)


def cube_kernel(
    dims,
    live_ref,
    domain_ref,
    grad_ref,
    act_ref,
    proj_ref,
    dom_down_ref,
    dom_up_ref,
    com_down_ref,
    com_up_ref,
    out_ref,
    down_grad_ref,
    up_grad_ref,
    sdown_ref,
    sup_ref,
    proj_other,
    masked_blocks,
    rows_all,
    up_all,
    down_map,
    low_send,
    low_recv,
    back_all,
    upg_send,
    upg_recv,
    sum_send,
    sum_recv,
    total_all,
    zl_send,
    zl_recv,
    kept,
    zh_send,
    zh_recv,
    proj_sems,
    rowz_sems,
    rowx_sems,
    rowc_sems,
    rowf_sems,
    up_sems,
    low_sems,
    back_sems,
    upg_sems,
    sum_sems,
    total_sems,
    zl_sems,
    zh_sems,
):
    n_dp, n_tensor, chunks = dims
    dp = lax.axis_index("dp")
    tensor = lax.axis_index("tensor")
    y = lax.rem(dp, 2)
    z = dp // 2
    rows, block = masked_blocks.shape[1], masked_blocks.shape[2]
    series_rows = rows * n_tensor
    rank, srank = dom_down_ref.shape[1], com_down_ref.shape[0]
    ranks = rank + srank
    domains = dom_down_ref.shape[0]
    width = act_ref.shape[1]
    per_tensor = width // block
    piece = width // n_dp

    def flip(index, bit):
        return index + bit - 2 * bit * lax.rem(index // bit, 2)

    def flips(index, mask):
        for bit in (1, 2, 4):
            if mask & bit:
                index = flip(index, bit)
        return index

    def copy(src, dst, sems, at, dp_to, tensor_to):
        return pltpu.make_async_remote_copy(
            src_ref=src,
            dst_ref=dst,
            send_sem=sems.at[0, at],
            recv_sem=sems.at[1, at],
            device_id=(dp_to, tensor_to),
            device_id_type=MESH,
        )

    barrier = pltpu.get_barrier_semaphore()
    for mask in range(1, n_dp):
        pl.semaphore_signal(barrier, inc=1, device_id=(flips(dp, mask), tensor), device_id_type=MESH)
    for mask in range(1, n_tensor):
        pl.semaphore_signal(barrier, inc=1, device_id=(dp, flips(tensor, mask)), device_id_type=MESH)
    pl.semaphore_wait(barrier, n_dp + n_tensor - 2)

    def proj_copy(c):
        at = pl.ds(pl.multiple_of(c * CHUNK, CHUNK), CHUNK)
        return copy(proj_ref.at[at], proj_other.at[at], proj_sems, c, flip(dp, 1), tensor)

    def row_z(m):
        zt = flips(z, m)
        return copy(
            masked_blocks.at[pl.ds(zt * 2, 2)],
            rows_all.at[m, tensor],
            rowz_sems,
            m - 1,
            zt * 2 + y,
            tensor,
        )

    def row_x(m):
        here = rows_all.at[m, tensor]
        return copy(here, here, rowx_sems, m, dp, flip(tensor, 2))

    def row_core(m):
        here = rows_all.at[m, tensor]
        return copy(here, here, rowc_sems, m, dp, flip(tensor, 1))

    def row_forward(m):
        here = rows_all.at[m, flip(tensor, 2)]
        return copy(here, here, rowf_sems, m, dp, flip(tensor, 1))

    def up_copy(m):
        here = up_all.at[tensor]
        return copy(here, here, up_sems, m - 1, dp, flips(tensor, m))

    def low_copy(m):
        to = flips(tensor, m)
        return copy(low_send.at[to], low_recv.at[m - 1], low_sems, m - 1, dp, to)

    def back_copy(m):
        here = back_all.at[tensor]
        return copy(here, here, back_sems, m - 1, dp, flips(tensor, m))

    def upg_copy(m):
        to = flips(tensor, m)
        return copy(upg_send.at[to], upg_recv.at[m - 1], upg_sems, m - 1, dp, to)

    def sum_copy(m):
        to = flips(dp, m)
        return copy(sum_send.at[to], sum_recv.at[dp], sum_sems, m - 1, to, tensor)

    def total_copy(held, bit):
        here = total_all.at[flips(dp, held)]
        return copy(here, here, total_sems, (held | bit) - 1, flip(dp, bit), tensor)

    def zl_copy(c):
        return copy(zl_send.at[c], zl_recv.at[c], zl_sems, c, flip(z, 1) * 2 + y, tensor)

    def zh_copy(c):
        return copy(zh_send.at[c], zh_recv.at[c], zh_sems, c, flip(z, 2) * 2 + y, tensor)

    @pl.loop(0, chunks)
    def _(c):
        proj_copy(c).start()

    live = live_ref[0]
    alive = tensor * rows + lax.broadcasted_iota(jnp.int32, (rows, block), 0) < live
    for j in range(masked_blocks.shape[0]):
        part = grad_ref[:, j * block : (j + 1) * block]
        masked_blocks[j] = jnp.where(alive, part, jnp.zeros_like(part))
    for m in (3, 2, 1):
        row_z(m).start()
    for h in range(2):
        rows_all[0, tensor, h] = masked_blocks[z * 2 + h]
    row_x(0).start()
    row_core(0).start()

    domain = domain_ref[dp]
    up_all[tensor, :rank] = dom_up_ref[domain]
    up_all[tensor, rank:] = com_up_ref[...]
    for m in range(1, n_tensor):
        up_copy(m).start()
    down_map[:rank] = dom_down_ref[domain]
    down_map[rank:] = com_down_ref[...]
    low_send[...] = jnp.zeros_like(low_send)
    back_all[tensor] = jnp.zeros_like(back_all.at[0])
    for j in range(n_tensor):
        low_send[j, :, :ranks] = nt_dot(act_ref[j * rows : (j + 1) * rows, :], down_map[...])
    for m in range(1, n_tensor):
        low_copy(m).start()

    for m in (1, 2, 3):
        row_z(m).wait_recv()
        row_x(m).start()
        row_core(m).start()

    for m in range(1, n_tensor):
        up_copy(m).wait_recv()
    back = jnp.zeros((rows, ranks), jnp.float32)
    for j in range(masked_blocks.shape[0]):
        at = (j % per_tensor) * block
        back += nt_dot(masked_blocks[j], up_all[j // per_tensor, :, at : at + block])
    back_all[tensor, :, :ranks] = back.astype(jnp.bfloat16)
    for m in range(1, n_tensor):
        back_copy(m).start()

    low = low_send[tensor]
    for m in range(1, n_tensor):
        low_copy(m).wait_recv()
        low += low_recv[m - 1]
    low_flip = low.astype(jnp.bfloat16).astype(jnp.float32).T.astype(jnp.bfloat16)
    for j in range(masked_blocks.shape[0]):
        at = (j % per_tensor) * block
        part = adapter_scale * jnp.dot(
            low_flip, masked_blocks[j], preferred_element_type=jnp.float32
        )
        upg_send[j // per_tensor, :, at : at + block] = part[:ranks]
    for m in range(1, n_tensor):
        upg_copy(m).start()

    for m in range(n_tensor):
        row_x(m).wait_recv()
        row_forward(m).start()

    for m in range(1, n_tensor):
        back_copy(m).wait_recv()
    lanes = back_all.shape[2]
    back_rows = back_all[...].reshape(series_rows, lanes)
    back_flip = back_rows.astype(jnp.float32).T.astype(jnp.bfloat16)
    for j in range(n_dp):
        at = slice(j * piece, (j + 1) * piece)
        part = adapter_scale * jnp.dot(
            back_flip, act_ref[:, at], preferred_element_type=jnp.float32
        )
        sum_send[j, :ranks] = part[:ranks].astype(jnp.bfloat16)
    for m in range(1, n_tensor):
        upg_copy(m).wait_recv()
    for j in range(n_dp):
        at = slice(j * piece, (j + 1) * piece)
        part = upg_send[tensor, :, at]
        for m in range(1, n_tensor):
            part += upg_recv[m - 1, :, at]
        sum_send[j, ranks:] = part.astype(jnp.bfloat16)
    for m in range(1, n_dp):
        sum_copy(m).start()
    sum_recv[dp] = sum_send[dp]

    for m in range(n_tensor):
        row_core(m).wait_recv()
        row_forward(m).wait_recv()

    def partial(m, c):
        at = pl.ds(pl.multiple_of(c * CHUNK, CHUNK), CHUNK)
        own = rows_all[m, :, y].reshape(series_rows, block)
        other = rows_all[m, :, 1 - y].reshape(series_rows, block)
        return nt_dot(own, proj_ref[at, :]) + nt_dot(other, proj_other[at, :])

    def add_totals():
        for m in range(1, n_dp):
            sum_copy(m).wait_recv()
        for kind in range(2):
            base = kind * ranks
            to = kind * (domains * rank + srank)
            shared = jnp.zeros((srank, piece), jnp.float32)
            for r in range(n_dp):
                shared += sum_recv[r, base + rank : base + ranks].astype(jnp.float32)
            for k in range(domains):
                total = jnp.zeros((rank, piece), jnp.float32)
                for r in range(n_dp):
                    term = sum_recv[r, base : base + rank].astype(jnp.float32)
                    total += jnp.where(domain_ref[r] == k, term, jnp.zeros_like(term))
                total_all[dp, to + k * rank : to + (k + 1) * rank] = total.astype(jnp.bfloat16)
            to += domains * rank
            total_all[dp, to : to + srank] = shared.astype(jnp.bfloat16)

    @pl.loop(0, chunks + 2)
    def _(c):
        @pl.when(c < chunks)
        def _():
            proj_copy(c).wait_recv()
            zl_send[c, 0] = partial(1, c).astype(jnp.bfloat16)
            zl_send[c, 1] = partial(3, c).astype(jnp.bfloat16)
            zl_copy(c).start()
            kept[c, 0] = partial(0, c)
            kept[c, 1] = partial(2, c)

        @pl.when(jnp.logical_and(c >= 1, c <= chunks))
        def _():
            b = c - 1
            zl_copy(b).wait_recv()
            zh_send[b] = (kept[b, 1] + zl_recv[b, 1].astype(jnp.float32)).astype(jnp.bfloat16)
            zh_copy(b).start()

        @pl.when(c >= 2)
        def _():
            a = c - 2
            at = pl.ds(pl.multiple_of(a * CHUNK, CHUNK), CHUNK)
            adapter = jnp.dot(
                back_all[...].reshape(series_rows, lanes)[:, :ranks],
                down_map[:, at],
                preferred_element_type=jnp.float32,
            )
            whole = kept[a, 0] + zl_recv[a, 0].astype(jnp.float32) + adapter_scale * adapter
            zh_copy(a).wait_recv()
            out_ref[:, at] = (whole + zh_recv[a].astype(jnp.float32)).astype(jnp.bfloat16)

        @pl.when(c == 1)
        def _():
            add_totals()
            total_copy(0, 4).start()

        @pl.when(c == 3)
        def _():
            total_copy(0, 4).wait_recv()
            for held in (0, 4):
                total_copy(held, 2).start()

        @pl.when(c == 5)
        def _():
            for held in (0, 4):
                total_copy(held, 2).wait_recv()
            for held in (0, 2, 4, 6):
                total_copy(held, 1).start()

    for held in (0, 2, 4, 6):
        total_copy(held, 1).wait_recv()
    side = domains * rank + srank
    for p in range(n_dp):
        at = slice(p * piece, (p + 1) * piece)
        for kind, dom_out, com_out in ((0, down_grad_ref, sdown_ref), (1, up_grad_ref, sup_ref)):
            for k in range(domains):
                first = kind * side + k * rank
                dom_out[k, :, at] = total_all[p, first : first + rank].astype(jnp.float32)
            first = kind * side + domains * rank
            com_out[:, at] = total_all[p, first : first + srank].astype(jnp.float32)

    @pl.loop(0, chunks)
    def _(c):
        proj_copy(c).wait_send()
        zl_copy(c).wait_send()
        zh_copy(c).wait_send()

    for m in (1, 2, 3):
        row_z(m).wait_send()
    for m in range(n_tensor):
        row_x(m).wait_send()
        row_core(m).wait_send()
        row_forward(m).wait_send()
    for m in range(1, n_tensor):
        up_copy(m).wait_send()
        low_copy(m).wait_send()
        back_copy(m).wait_send()
        upg_copy(m).wait_send()
    for m in range(1, n_dp):
        sum_copy(m).wait_send()
    for bit, helds in ((4, (0,)), (2, (0, 4)), (1, (0, 2, 4, 6))):
        for held in helds:
            total_copy(held, bit).wait_send()


def on_cube(
    n_dp,
    n_tensor,
    output_gradient,
    attention_output,
    frozen_projection,
    domain_down_map,
    domain_up_map,
    common_down_map,
    common_up_map,
    live_token_count,
    series_domain,
):
    rows, model = output_gradient.shape
    series_rows, width = attention_output.shape
    block = frozen_projection.shape[1]
    domains, rank = domain_down_map.shape[:2]
    srank = common_down_map.shape[0]
    ranks, side = rank + srank, domains * rank + srank
    chunks, piece, blocks = width // CHUNK, width // n_dp, model // block
    lanes = 128
    bf16, f32 = jnp.bfloat16, jnp.float32
    vmem = pl.BlockSpec(memory_space=pltpu.VMEM)
    smem = pl.BlockSpec(memory_space=pltpu.SMEM)

    def sems(count):
        return pltpu.SemaphoreType.DMA((2, count))

    return pl.pallas_call(
        functools.partial(cube_kernel, (n_dp, n_tensor, chunks)),
        out_shape=(
            jax.ShapeDtypeStruct((series_rows, width), bf16),
            jax.ShapeDtypeStruct((domains, rank, width), f32),
            jax.ShapeDtypeStruct((domains, rank, width), f32),
            jax.ShapeDtypeStruct((srank, width), f32),
            jax.ShapeDtypeStruct((srank, width), f32),
        ),
        in_specs=[smem] * 2 + [vmem] * 7,
        out_specs=(vmem,) * 5,
        scratch_shapes=[
            pltpu.VMEM((width, block), bf16),
            pltpu.VMEM((blocks, rows, block), bf16),
            pltpu.VMEM((4, n_tensor, 2, rows, block), bf16),
            pltpu.VMEM((n_tensor, ranks, width), bf16),
            pltpu.VMEM((ranks, width), bf16),
            pltpu.VMEM((n_tensor, rows, lanes), f32),
            pltpu.VMEM((n_tensor - 1, rows, lanes), f32),
            pltpu.VMEM((n_tensor, rows, lanes), bf16),
            pltpu.VMEM((n_tensor, ranks, width), f32),
            pltpu.VMEM((n_tensor - 1, ranks, width), f32),
            pltpu.VMEM((n_dp, 2 * ranks, piece), bf16),
            pltpu.VMEM((n_dp, 2 * ranks, piece), bf16),
            pltpu.VMEM((n_dp, 2 * side, piece), bf16),
            pltpu.VMEM((chunks, 2, series_rows, CHUNK), bf16),
            pltpu.VMEM((chunks, 2, series_rows, CHUNK), bf16),
            pltpu.VMEM((chunks, 2, series_rows, CHUNK), f32),
            pltpu.VMEM((chunks, series_rows, CHUNK), bf16),
            pltpu.VMEM((chunks, series_rows, CHUNK), bf16),
            sems(chunks),
            sems(3),
            sems(n_tensor),
            sems(n_tensor),
            sems(n_tensor),
            sems(n_tensor - 1),
            sems(n_tensor - 1),
            sems(n_tensor - 1),
            sems(n_tensor - 1),
            sems(n_dp - 1),
            sems(n_dp - 1),
            sems(chunks),
            sems(chunks),
        ],
        compiler_params=pltpu.CompilerParams(
            collective_id=0, has_side_effects=True, vmem_limit_bytes=60 * 1024 * 1024
        ),
    )(
        live_token_count,
        series_domain,
        output_gradient,
        attention_output,
        frozen_projection,
        domain_down_map,
        domain_up_map,
        common_down_map,
        common_up_map,
    )


def solution(mesh):
    placed = (
        P(("dp", "tensor"), None),
        P("dp", "tensor"),
        P("tensor", "dp"),
        P(None, None, "tensor"),
        P(None, None, "tensor"),
        P(None, "tensor"),
        P(None, "tensor"),
        P("dp"),
        P(),
    )
    n_dp, n_tensor = mesh.shape["dp"], mesh.shape["tensor"]
    on_one = on_device
    if n_dp == 2**3 and n_tensor == 2**2:
        on_one = functools.partial(on_cube, n_dp, n_tensor)
    return jax.shard_map(
        on_one,
        mesh=mesh,
        in_specs=placed,
        out_specs=(
            P("dp", "tensor"),
            P(None, None, "tensor"),
            P(None, None, "tensor"),
            P(None, "tensor"),
            P(None, "tensor"),
        ),
        check_vma=False,
    )
```

```python
import functools

import jax
import jax.numpy as jnp
from jax import lax
from jax.experimental import pallas as pl
from jax.experimental.pallas import tpu as pltpu
from jax.sharding import PartitionSpec as P

adapter_scale = 2.0
shared_scale = 2.0
contract_dims = (((1,), (1,)), ((), ()))
outer_dims = (((0,), (0,)), ((), ()))


def on_device(
    output_gradient,
    attention_output,
    frozen_projection,
    domain_down_map,
    domain_up_map,
    common_down_map,
    common_up_map,
    live_token_count,
    series_domain,
):
    rows_local = output_gradient.shape[0]
    tensor_index = lax.axis_index("tensor")
    rank_index = lax.axis_index("dp")
    domain_number = lax.dynamic_index_in_dim(series_domain, rank_index, 0, keepdims=False)
    local_down_map = lax.dynamic_index_in_dim(domain_down_map, domain_number, 0, keepdims=False)
    local_up_map = lax.dynamic_index_in_dim(domain_up_map, domain_number, 0, keepdims=False)
    positions = tensor_index * rows_local + lax.iota(jnp.int32, rows_local)
    live_rows = (positions < live_token_count[0])[:, None]
    masked = jnp.where(live_rows, output_gradient, jnp.zeros_like(output_gradient))
    down_part = lax.dot_general(
        attention_output, local_down_map, contract_dims, preferred_element_type=jnp.float32
    )
    shared_part = lax.dot_general(
        attention_output, common_down_map, contract_dims, preferred_element_type=jnp.float32
    )
    down_total, shared_total = lax.psum((down_part, shared_part), "tensor")
    reduced_activation = down_total.astype(jnp.bfloat16)
    low_shared = shared_total.astype(jnp.bfloat16)
    gathered = lax.all_gather(masked, "tensor", axis=0, tiled=True)
    column_width = local_up_map.shape[1]
    my_columns = lax.dynamic_slice_in_dim(gathered, tensor_index * column_width, column_width, 1)
    dom_partial = lax.dot_general(
        my_columns, local_up_map, contract_dims, preferred_element_type=jnp.float32
    )
    shared_partial = lax.dot_general(
        my_columns, common_up_map, contract_dims, preferred_element_type=jnp.float32
    )
    dom_total, shared_back_total = lax.psum((dom_partial, shared_partial), "tensor")
    domain_backward = dom_total.astype(jnp.bfloat16)
    back_shared = shared_back_total.astype(jnp.bfloat16)
    local_down_gradient = adapter_scale * lax.dot_general(
        domain_backward, attention_output, outer_dims, preferred_element_type=jnp.float32
    )
    local_up_gradient = adapter_scale * lax.dot_general(
        reduced_activation, my_columns, outer_dims, preferred_element_type=jnp.float32
    )
    grad_sdown = shared_scale * lax.dot_general(
        back_shared, attention_output, outer_dims, preferred_element_type=jnp.float32
    )
    grad_sup = shared_scale * lax.dot_general(
        low_shared, my_columns, outer_dims, preferred_element_type=jnp.float32
    )
    domain_picker = (lax.iota(jnp.int32, domain_down_map.shape[0]) == domain_number).astype(
        jnp.float32
    )[:, None, None]
    frozen_total = lax.dot_general(
        gathered,
        lax.all_gather(frozen_projection, "dp", axis=1, tiled=True),
        contract_dims,
        preferred_element_type=jnp.float32,
    )
    summed = lax.psum(
        (
            domain_picker * local_down_gradient[None],
            domain_picker * local_up_gradient[None],
            grad_sdown,
            grad_sup,
        ),
        "dp",
    )
    adapter_contribution = adapter_scale * jnp.dot(
        domain_backward, local_down_map, preferred_element_type=jnp.float32
    )
    adapter_contribution = adapter_contribution + shared_scale * jnp.dot(
        back_shared, common_down_map, preferred_element_type=jnp.float32
    )
    grad_input = (frozen_total + adapter_contribution).astype(jnp.bfloat16)
    return (grad_input, summed[0], summed[1], summed[2], summed[3])

MESH = pl.DeviceIdType.MESH
CHUNK = 256
AHEAD = 2


def nt_dot(left, right):
    return lax.dot_general(left, right, contract_dims, preferred_element_type=jnp.float32)


def cube_kernel(
    dims,
    live_ref,
    domain_ref,
    grad_ref,
    act_ref,
    proj_ref,
    dom_down_ref,
    dom_up_ref,
    com_down_ref,
    com_up_ref,
    out_ref,
    down_grad_ref,
    up_grad_ref,
    sdown_ref,
    sup_ref,
    proj_other,
    masked_blocks,
    rows_all,
    up_all,
    down_map,
    low_send,
    low_recv,
    back_all,
    upg_send,
    upg_recv,
    sum_send,
    sum_recv,
    total_all,
    zl_send,
    zl_recv,
    kept,
    zh_send,
    zh_recv,
    proj_sems,
    rowz_sems,
    rowx_sems,
    rowc_sems,
    rowf_sems,
    up_sems,
    low_sems,
    back_sems,
    upg_sems,
    sum_sems,
    total_sems,
    zl_sems,
    zh_sems,
):
    n_dp, n_tensor, chunks = dims
    dp = lax.axis_index("dp")
    tensor = lax.axis_index("tensor")
    y = lax.rem(dp, 2)
    z = dp // 2
    rows, block = masked_blocks.shape[1], masked_blocks.shape[2]
    series_rows = rows * n_tensor
    rank, srank = dom_down_ref.shape[1], com_down_ref.shape[0]
    ranks = rank + srank
    domains = dom_down_ref.shape[0]
    width = act_ref.shape[1]
    per_tensor = width // block
    piece = width // n_dp

    def flip(index, bit):
        return index + bit - 2 * bit * lax.rem(index // bit, 2)

    def flips(index, mask):
        for bit in (1, 2, 4):
            if mask & bit:
                index = flip(index, bit)
        return index

    def copy(src, dst, sems, at, dp_to, tensor_to):
        return pltpu.make_async_remote_copy(
            src_ref=src,
            dst_ref=dst,
            send_sem=sems.at[0, at],
            recv_sem=sems.at[1, at],
            device_id=(dp_to, tensor_to),
            device_id_type=MESH,
        )

    barrier = pltpu.get_barrier_semaphore()
    for mask in range(1, n_dp):
        pl.semaphore_signal(barrier, inc=1, device_id=(flips(dp, mask), tensor), device_id_type=MESH)
    for mask in range(1, n_tensor):
        pl.semaphore_signal(barrier, inc=1, device_id=(dp, flips(tensor, mask)), device_id_type=MESH)
    pl.semaphore_wait(barrier, n_dp + n_tensor - 2)

    def proj_copy(c):
        at = pl.ds(pl.multiple_of(c * CHUNK, CHUNK), CHUNK)
        return copy(proj_ref.at[at], proj_other.at[at], proj_sems, c, flip(dp, 1), tensor)

    def row_z(m):
        zt = flips(z, m)
        return copy(
            masked_blocks.at[pl.ds(zt * 2, 2)],
            rows_all.at[m, tensor],
            rowz_sems,
            m - 1,
            zt * 2 + y,
            tensor,
        )

    def row_x(m):
        here = rows_all.at[m, tensor]
        return copy(here, here, rowx_sems, m, dp, flip(tensor, 2))

    def row_core(m):
        here = rows_all.at[m, tensor]
        return copy(here, here, rowc_sems, m, dp, flip(tensor, 1))

    def row_forward(m):
        here = rows_all.at[m, flip(tensor, 2)]
        return copy(here, here, rowf_sems, m, dp, flip(tensor, 1))

    def up_copy(m):
        here = up_all.at[tensor]
        return copy(here, here, up_sems, m - 1, dp, flips(tensor, m))

    def low_copy(m):
        to = flips(tensor, m)
        return copy(low_send.at[to], low_recv.at[m - 1], low_sems, m - 1, dp, to)

    def back_copy(m):
        here = back_all.at[tensor]
        return copy(here, here, back_sems, m - 1, dp, flips(tensor, m))

    def upg_copy(m):
        to = flips(tensor, m)
        return copy(upg_send.at[to], upg_recv.at[m - 1], upg_sems, m - 1, dp, to)

    def sum_copy(m):
        to = flips(dp, m)
        return copy(sum_send.at[to], sum_recv.at[dp], sum_sems, m - 1, to, tensor)

    def total_copy(held, bit):
        here = total_all.at[flips(dp, held)]
        return copy(here, here, total_sems, (held | bit) - 1, flip(dp, bit), tensor)

    def zl_copy(k, c):
        part_of = zl_send.at[c, k]
        return copy(part_of, zl_recv.at[c, k], zl_sems, 2 * c + k, flip(z, 1) * 2 + y, tensor)

    def zh_copy(c):
        return copy(zh_send.at[c], zh_recv.at[c], zh_sems, c, flip(z, 2) * 2 + y, tensor)

    def partial(m, c):
        at = pl.ds(pl.multiple_of(c * CHUNK, CHUNK), CHUNK)
        own = rows_all[m, :, y].reshape(series_rows, block)
        other = rows_all[m, :, 1 - y].reshape(series_rows, block)
        return nt_dot(own, proj_ref[at, :]) + nt_dot(other, proj_other[at, :])

    def take_proj(c):
        proj_copy(c).wait_recv()

        @pl.when(c + AHEAD < chunks)
        def _():
            proj_copy(c).wait_send()
            proj_copy(c + AHEAD).start()

    def send_partial(k, c):
        zl_send[c, k] = partial(2 * k + 1, c).astype(jnp.bfloat16)
        zl_copy(k, c).start()

    def finish_rows(m):
        row_x(m).wait_recv()
        row_forward(m).start()
        row_core(m).wait_recv()
        row_forward(m).wait_recv()

    for c in range(AHEAD):
        proj_copy(c).start()

    live = live_ref[0]
    alive = tensor * rows + lax.broadcasted_iota(jnp.int32, (rows, block), 0) < live
    for j in range(masked_blocks.shape[0]):
        part = grad_ref[:, j * block : (j + 1) * block]
        masked_blocks[j] = jnp.where(alive, part, jnp.zeros_like(part))
    row_z(1).start()
    for h in range(2):
        rows_all[0, tensor, h] = masked_blocks[z * 2 + h]
    row_x(0).start()
    row_core(0).start()

    domain = domain_ref[dp]
    up_all[tensor, :rank] = dom_up_ref[domain]
    up_all[tensor, rank:] = com_up_ref[...]
    down_map[:rank] = dom_down_ref[domain]
    down_map[rank:] = com_down_ref[...]
    low_send[...] = jnp.zeros_like(low_send)
    back_all[tensor] = jnp.zeros_like(back_all.at[0])
    for j in range(n_tensor):
        low_send[j, :, :ranks] = nt_dot(act_ref[j * rows : (j + 1) * rows, :], down_map[...])

    row_z(1).wait_send()
    row_z(3).start()
    row_z(1).wait_recv()
    row_x(1).start()
    row_core(1).start()
    for m in range(1, n_tensor):
        up_copy(m).start()
        low_copy(m).start()
    row_x(0).wait_recv()
    row_forward(0).start()
    finish_rows(1)

    take_proj(0)
    send_partial(0, 0)
    row_z(3).wait_send()
    row_z(2).start()
    take_proj(1)
    send_partial(0, 1)

    row_z(3).wait_recv()
    row_x(3).start()
    row_core(3).start()

    for m in range(1, n_tensor):
        up_copy(m).wait_recv()
    back = jnp.zeros((rows, ranks), jnp.float32)
    for j in range(masked_blocks.shape[0]):
        at = (j % per_tensor) * block
        back += nt_dot(masked_blocks[j], up_all[j // per_tensor, :, at : at + block])
    back_all[tensor, :, :ranks] = back.astype(jnp.bfloat16)
    for m in range(1, n_tensor):
        back_copy(m).start()

    low = low_send[tensor]
    for m in range(1, n_tensor):
        low_copy(m).wait_recv()
        low += low_recv[m - 1]
    low_flip = low.astype(jnp.bfloat16).astype(jnp.float32).T.astype(jnp.bfloat16)
    for j in range(masked_blocks.shape[0]):
        at = (j % per_tensor) * block
        part = adapter_scale * jnp.dot(
            low_flip, masked_blocks[j], preferred_element_type=jnp.float32
        )
        upg_send[j // per_tensor, :, at : at + block] = part[:ranks]

    finish_rows(3)
    send_partial(1, 0)
    send_partial(1, 1)
    take_proj(2)
    send_partial(0, 2)
    send_partial(1, 2)
    row_z(2).wait_recv()
    row_x(2).start()
    row_core(2).start()
    for m in range(1, n_tensor):
        upg_copy(m).start()
    take_proj(3)
    send_partial(0, 3)
    send_partial(1, 3)
    finish_rows(2)
    row_core(0).wait_recv()
    row_forward(0).wait_recv()
    early = 4

    lanes = back_all.shape[2]

    def send_sums():
        for m in range(1, n_tensor):
            back_copy(m).wait_recv()
        back_rows = back_all[...].reshape(series_rows, lanes)
        back_flip = back_rows.astype(jnp.float32).T.astype(jnp.bfloat16)
        for j in range(n_dp):
            at = slice(j * piece, (j + 1) * piece)
            part = adapter_scale * jnp.dot(
                back_flip, act_ref[:, at], preferred_element_type=jnp.float32
            )
            sum_send[j, :ranks] = part[:ranks].astype(jnp.bfloat16)
        for m in range(1, n_tensor):
            upg_copy(m).wait_recv()
        for j in range(n_dp):
            at = slice(j * piece, (j + 1) * piece)
            part = upg_send[tensor, :, at]
            for m in range(1, n_tensor):
                part += upg_recv[m - 1, :, at]
            sum_send[j, ranks:] = part.astype(jnp.bfloat16)
        for m in range(1, n_dp):
            sum_copy(m).start()
        sum_recv[dp] = sum_send[dp]

    def add_totals():
        for m in range(1, n_dp):
            sum_copy(m).wait_recv()
        for kind in range(2):
            base = kind * ranks
            to = kind * (domains * rank + srank)
            shared = jnp.zeros((srank, piece), jnp.float32)
            for r in range(n_dp):
                shared += sum_recv[r, base + rank : base + ranks].astype(jnp.float32)
            for k in range(domains):
                total = jnp.zeros((rank, piece), jnp.float32)
                for r in range(n_dp):
                    term = sum_recv[r, base : base + rank].astype(jnp.float32)
                    total += jnp.where(domain_ref[r] == k, term, jnp.zeros_like(term))
                total_all[dp, to + k * rank : to + (k + 1) * rank] = total.astype(jnp.bfloat16)
            to += domains * rank
            total_all[dp, to : to + srank] = shared.astype(jnp.bfloat16)

    def write_totals():
        side = domains * rank + srank
        for p in range(n_dp):
            at = slice(p * piece, (p + 1) * piece)
            for kind, dom_out, com_out in ((0, down_grad_ref, sdown_ref), (1, up_grad_ref, sup_ref)):
                for k in range(domains):
                    first = kind * side + k * rank
                    dom_out[k, :, at] = total_all[p, first : first + rank].astype(jnp.float32)
                first = kind * side + domains * rank
                com_out[:, at] = total_all[p, first : first + srank].astype(jnp.float32)

    @pl.loop(0, chunks + 2)
    def _(c):
        @pl.when(jnp.logical_and(c >= early, c < chunks))
        def _():
            take_proj(c)
            send_partial(0, c)
            send_partial(1, c)

        @pl.when(c < chunks)
        def _():
            kept[c, 1] = partial(2, c)
            kept[c, 0] = partial(0, c)

        @pl.when(jnp.logical_and(c >= 1, c <= chunks))
        def _():
            b = c - 1
            zl_copy(1, b).wait_recv()
            zh_send[b] = (kept[b, 1] + zl_recv[b, 1].astype(jnp.float32)).astype(jnp.bfloat16)
            zh_copy(b).start()

        @pl.when(c >= 2)
        def _():
            a = c - 2
            at = pl.ds(pl.multiple_of(a * CHUNK, CHUNK), CHUNK)
            adapter = jnp.dot(
                back_all[...].reshape(series_rows, lanes)[:, :ranks],
                down_map[:, at],
                preferred_element_type=jnp.float32,
            )
            zl_copy(0, a).wait_recv()
            whole = kept[a, 0] + zl_recv[a, 0].astype(jnp.float32) + adapter_scale * adapter
            zh_copy(a).wait_recv()
            out_ref[:, at] = (whole + zh_recv[a].astype(jnp.float32)).astype(jnp.bfloat16)

        @pl.when(c == 0)
        def _():
            send_sums()

        @pl.when(c == 2)
        def _():
            add_totals()
            total_copy(0, 4).start()

        @pl.when(c == 4)
        def _():
            total_copy(0, 4).wait_recv()
            for held in (0, 4):
                total_copy(held, 2).start()

        @pl.when(c == 6)
        def _():
            for held in (0, 4):
                total_copy(held, 2).wait_recv()
            for held in (0, 2, 4, 6):
                total_copy(held, 1).start()

        @pl.when(c == chunks)
        def _():
            for held in (0, 2, 4, 6):
                total_copy(held, 1).wait_recv()
            write_totals()

    @pl.loop(0, chunks)
    def _(c):
        zl_copy(0, c).wait_send()
        zl_copy(1, c).wait_send()
        zh_copy(c).wait_send()

    for c in range(AHEAD):
        proj_copy(chunks - AHEAD + c).wait_send()
    row_z(2).wait_send()
    for m in range(n_tensor):
        row_x(m).wait_send()
        row_core(m).wait_send()
        row_forward(m).wait_send()
    for m in range(1, n_tensor):
        up_copy(m).wait_send()
        low_copy(m).wait_send()
        back_copy(m).wait_send()
        upg_copy(m).wait_send()
    for m in range(1, n_dp):
        sum_copy(m).wait_send()
    for bit, helds in ((4, (0,)), (2, (0, 4)), (1, (0, 2, 4, 6))):
        for held in helds:
            total_copy(held, bit).wait_send()


def on_cube(
    n_dp,
    n_tensor,
    output_gradient,
    attention_output,
    frozen_projection,
    domain_down_map,
    domain_up_map,
    common_down_map,
    common_up_map,
    live_token_count,
    series_domain,
):
    rows, model = output_gradient.shape
    series_rows, width = attention_output.shape
    block = frozen_projection.shape[1]
    domains, rank = domain_down_map.shape[:2]
    srank = common_down_map.shape[0]
    ranks, side = rank + srank, domains * rank + srank
    chunks, piece, blocks = width // CHUNK, width // n_dp, model // block
    lanes = 128
    bf16, f32 = jnp.bfloat16, jnp.float32
    vmem = pl.BlockSpec(memory_space=pltpu.VMEM)
    smem = pl.BlockSpec(memory_space=pltpu.SMEM)

    def sems(count):
        return pltpu.SemaphoreType.DMA((2, count))

    return pl.pallas_call(
        functools.partial(cube_kernel, (n_dp, n_tensor, chunks)),
        out_shape=(
            jax.ShapeDtypeStruct((series_rows, width), bf16),
            jax.ShapeDtypeStruct((domains, rank, width), f32),
            jax.ShapeDtypeStruct((domains, rank, width), f32),
            jax.ShapeDtypeStruct((srank, width), f32),
            jax.ShapeDtypeStruct((srank, width), f32),
        ),
        in_specs=[smem] * 2 + [vmem] * 7,
        out_specs=(vmem,) * 5,
        scratch_shapes=[
            pltpu.VMEM((width, block), bf16),
            pltpu.VMEM((blocks, rows, block), bf16),
            pltpu.VMEM((4, n_tensor, 2, rows, block), bf16),
            pltpu.VMEM((n_tensor, ranks, width), bf16),
            pltpu.VMEM((ranks, width), bf16),
            pltpu.VMEM((n_tensor, rows, lanes), f32),
            pltpu.VMEM((n_tensor - 1, rows, lanes), f32),
            pltpu.VMEM((n_tensor, rows, lanes), bf16),
            pltpu.VMEM((n_tensor, ranks, width), f32),
            pltpu.VMEM((n_tensor - 1, ranks, width), f32),
            pltpu.VMEM((n_dp, 2 * ranks, piece), bf16),
            pltpu.VMEM((n_dp, 2 * ranks, piece), bf16),
            pltpu.VMEM((n_dp, 2 * side, piece), bf16),
            pltpu.VMEM((chunks, 2, series_rows, CHUNK), bf16),
            pltpu.VMEM((chunks, 2, series_rows, CHUNK), bf16),
            pltpu.VMEM((chunks, 2, series_rows, CHUNK), f32),
            pltpu.VMEM((chunks, series_rows, CHUNK), bf16),
            pltpu.VMEM((chunks, series_rows, CHUNK), bf16),
            sems(chunks),
            sems(3),
            sems(n_tensor),
            sems(n_tensor),
            sems(n_tensor),
            sems(n_tensor - 1),
            sems(n_tensor - 1),
            sems(n_tensor - 1),
            sems(n_tensor - 1),
            sems(n_dp - 1),
            sems(n_dp - 1),
            sems(2 * chunks),
            sems(chunks),
        ],
        compiler_params=pltpu.CompilerParams(
            collective_id=0, has_side_effects=True, vmem_limit_bytes=60 * 1024 * 1024
        ),
    )(
        live_token_count,
        series_domain,
        output_gradient,
        attention_output,
        frozen_projection,
        domain_down_map,
        domain_up_map,
        common_down_map,
        common_up_map,
    )


def solution(mesh):
    placed = (
        P(("dp", "tensor"), None),
        P("dp", "tensor"),
        P("tensor", "dp"),
        P(None, None, "tensor"),
        P(None, None, "tensor"),
        P(None, "tensor"),
        P(None, "tensor"),
        P("dp"),
        P(),
    )
    n_dp, n_tensor = mesh.shape["dp"], mesh.shape["tensor"]
    on_one = on_device
    if n_dp == 2**3 and n_tensor == 2**2:
        on_one = functools.partial(on_cube, n_dp, n_tensor)
    return jax.shard_map(
        on_one,
        mesh=mesh,
        in_specs=placed,
        out_specs=(
            P("dp", "tensor"),
            P(None, None, "tensor"),
            P(None, None, "tensor"),
            P(None, "tensor"),
            P(None, "tensor"),
        ),
        check_vma=False,
    )
```

```python
import functools

import jax
import jax.numpy as jnp
from jax import lax
from jax.experimental import pallas as pl
from jax.experimental.pallas import tpu as pltpu
from jax.sharding import PartitionSpec as P

adapter_scale = 2.0
shared_scale = 2.0
contract_dims = (((1,), (1,)), ((), ()))
outer_dims = (((0,), (0,)), ((), ()))


def on_device(
    output_gradient,
    attention_output,
    frozen_projection,
    domain_down_map,
    domain_up_map,
    common_down_map,
    common_up_map,
    live_token_count,
    series_domain,
):
    rows_local = output_gradient.shape[0]
    tensor_index = lax.axis_index("tensor")
    rank_index = lax.axis_index("dp")
    domain_number = lax.dynamic_index_in_dim(series_domain, rank_index, 0, keepdims=False)
    local_down_map = lax.dynamic_index_in_dim(domain_down_map, domain_number, 0, keepdims=False)
    local_up_map = lax.dynamic_index_in_dim(domain_up_map, domain_number, 0, keepdims=False)
    positions = tensor_index * rows_local + lax.iota(jnp.int32, rows_local)
    live_rows = (positions < live_token_count[0])[:, None]
    masked = jnp.where(live_rows, output_gradient, jnp.zeros_like(output_gradient))
    down_part = lax.dot_general(
        attention_output, local_down_map, contract_dims, preferred_element_type=jnp.float32
    )
    shared_part = lax.dot_general(
        attention_output, common_down_map, contract_dims, preferred_element_type=jnp.float32
    )
    down_total, shared_total = lax.psum((down_part, shared_part), "tensor")
    reduced_activation = down_total.astype(jnp.bfloat16)
    low_shared = shared_total.astype(jnp.bfloat16)
    gathered = lax.all_gather(masked, "tensor", axis=0, tiled=True)
    column_width = local_up_map.shape[1]
    my_columns = lax.dynamic_slice_in_dim(gathered, tensor_index * column_width, column_width, 1)
    dom_partial = lax.dot_general(
        my_columns, local_up_map, contract_dims, preferred_element_type=jnp.float32
    )
    shared_partial = lax.dot_general(
        my_columns, common_up_map, contract_dims, preferred_element_type=jnp.float32
    )
    dom_total, shared_back_total = lax.psum((dom_partial, shared_partial), "tensor")
    domain_backward = dom_total.astype(jnp.bfloat16)
    back_shared = shared_back_total.astype(jnp.bfloat16)
    local_down_gradient = adapter_scale * lax.dot_general(
        domain_backward, attention_output, outer_dims, preferred_element_type=jnp.float32
    )
    local_up_gradient = adapter_scale * lax.dot_general(
        reduced_activation, my_columns, outer_dims, preferred_element_type=jnp.float32
    )
    grad_sdown = shared_scale * lax.dot_general(
        back_shared, attention_output, outer_dims, preferred_element_type=jnp.float32
    )
    grad_sup = shared_scale * lax.dot_general(
        low_shared, my_columns, outer_dims, preferred_element_type=jnp.float32
    )
    domain_picker = (lax.iota(jnp.int32, domain_down_map.shape[0]) == domain_number).astype(
        jnp.float32
    )[:, None, None]
    frozen_total = lax.dot_general(
        gathered,
        lax.all_gather(frozen_projection, "dp", axis=1, tiled=True),
        contract_dims,
        preferred_element_type=jnp.float32,
    )
    summed = lax.psum(
        (
            domain_picker * local_down_gradient[None],
            domain_picker * local_up_gradient[None],
            grad_sdown,
            grad_sup,
        ),
        "dp",
    )
    adapter_contribution = adapter_scale * jnp.dot(
        domain_backward, local_down_map, preferred_element_type=jnp.float32
    )
    adapter_contribution = adapter_contribution + shared_scale * jnp.dot(
        back_shared, common_down_map, preferred_element_type=jnp.float32
    )
    grad_input = (frozen_total + adapter_contribution).astype(jnp.bfloat16)
    return (grad_input, summed[0], summed[1], summed[2], summed[3])

MESH = pl.DeviceIdType.MESH
CHUNK = 256
AHEAD = 3


def nt_dot(left, right):
    return lax.dot_general(left, right, contract_dims, preferred_element_type=jnp.float32)


def cube_kernel(
    dims,
    live_ref,
    domain_ref,
    grad_ref,
    act_ref,
    proj_ref,
    dom_down_ref,
    dom_up_ref,
    com_down_ref,
    com_up_ref,
    out_ref,
    down_grad_ref,
    up_grad_ref,
    sdown_ref,
    sup_ref,
    proj_other,
    masked_blocks,
    rows_all,
    up_all,
    down_map,
    low_send,
    low_recv,
    back_all,
    upg_send,
    upg_recv,
    sum_send,
    sum_recv,
    total_all,
    zl_send,
    zl_recv,
    kept,
    zh_send,
    zh_recv,
    proj_sems,
    rowz_sems,
    rowx_sems,
    rowc_sems,
    rowf_sems,
    up_sems,
    low_sems,
    back_sems,
    upg_sems,
    sum_sems,
    total_sems,
    zl_sems,
    zh_sems,
):
    n_dp, n_tensor, chunks = dims
    dp = lax.axis_index("dp")
    tensor = lax.axis_index("tensor")
    y = lax.rem(dp, 2)
    z = dp // 2
    rows, block = masked_blocks.shape[1], masked_blocks.shape[2]
    series_rows = rows * n_tensor
    rank, srank = dom_down_ref.shape[1], com_down_ref.shape[0]
    ranks = rank + srank
    domains = dom_down_ref.shape[0]
    width = act_ref.shape[1]
    per_tensor = width // block
    piece = width // n_dp

    def flip(index, bit):
        return index + bit - 2 * bit * lax.rem(index // bit, 2)

    def flips(index, mask):
        for bit in (1, 2, 4):
            if mask & bit:
                index = flip(index, bit)
        return index

    def copy(src, dst, sems, at, dp_to, tensor_to):
        return pltpu.make_async_remote_copy(
            src_ref=src,
            dst_ref=dst,
            send_sem=sems.at[0, at],
            recv_sem=sems.at[1, at],
            device_id=(dp_to, tensor_to),
            device_id_type=MESH,
        )

    barrier = pltpu.get_barrier_semaphore()
    for mask in range(1, n_dp):
        pl.semaphore_signal(barrier, inc=1, device_id=(flips(dp, mask), tensor), device_id_type=MESH)
    for mask in range(1, n_tensor):
        pl.semaphore_signal(barrier, inc=1, device_id=(dp, flips(tensor, mask)), device_id_type=MESH)
    pl.semaphore_wait(barrier, n_dp + n_tensor - 2)

    def proj_copy(c):
        at = pl.ds(pl.multiple_of(c * CHUNK, CHUNK), CHUNK)
        return copy(proj_ref.at[at], proj_other.at[at], proj_sems, c, flip(dp, 1), tensor)

    def row_z(m):
        zt = flips(z, m)
        return copy(
            masked_blocks.at[pl.ds(zt * 2, 2)],
            rows_all.at[m, tensor],
            rowz_sems,
            m - 1,
            zt * 2 + y,
            tensor,
        )

    def row_x(m):
        here = rows_all.at[m, tensor]
        return copy(here, here, rowx_sems, m, dp, flip(tensor, 2))

    def row_core(m):
        here = rows_all.at[m, tensor]
        return copy(here, here, rowc_sems, m, dp, flip(tensor, 1))

    def row_forward(m):
        here = rows_all.at[m, flip(tensor, 2)]
        return copy(here, here, rowf_sems, m, dp, flip(tensor, 1))

    def up_copy(m):
        here = up_all.at[tensor]
        return copy(here, here, up_sems, m - 1, dp, flips(tensor, m))

    def low_copy(m):
        to = flips(tensor, m)
        return copy(low_send.at[to], low_recv.at[m - 1], low_sems, m - 1, dp, to)

    def back_copy(m):
        here = back_all.at[tensor]
        return copy(here, here, back_sems, m - 1, dp, flips(tensor, m))

    def upg_copy(m):
        to = flips(tensor, m)
        return copy(upg_send.at[to], upg_recv.at[m - 1], upg_sems, m - 1, dp, to)

    def sum_copy(m):
        to = flips(dp, m)
        return copy(sum_send.at[to], sum_recv.at[dp], sum_sems, m - 1, to, tensor)

    def total_copy(held, bit):
        here = total_all.at[flips(dp, held)]
        return copy(here, here, total_sems, (held | bit) - 1, flip(dp, bit), tensor)

    def zl_copy(k, c):
        part_of = zl_send.at[c, k]
        return copy(part_of, zl_recv.at[c, k], zl_sems, 2 * c + k, flip(z, 1) * 2 + y, tensor)

    def zh_copy(c):
        return copy(zh_send.at[c], zh_recv.at[c], zh_sems, c, flip(z, 2) * 2 + y, tensor)

    def partial(m, c):
        at = pl.ds(pl.multiple_of(c * CHUNK, CHUNK), CHUNK)
        own = rows_all[m, :, y].reshape(series_rows, block)
        other = rows_all[m, :, 1 - y].reshape(series_rows, block)
        return nt_dot(own, proj_ref[at, :]) + nt_dot(other, proj_other[at, :])

    def take_proj(c):
        proj_copy(c).wait_recv()

        proj_copy(c).wait_send()

        @pl.when(c + AHEAD < chunks)
        def _():
            proj_copy(c + AHEAD).start()

    def send_partial(k, c):
        zl_send[c, k] = partial(2 * k + 1, c).astype(jnp.bfloat16)
        zl_copy(k, c).start()

    def finish_rows(m):
        row_x(m).wait_recv()
        row_forward(m).start()
        row_core(m).wait_recv()
        row_forward(m).wait_recv()

    for c in range(AHEAD - 1):
        proj_copy(c).start()

    live = live_ref[0]
    alive = tensor * rows + lax.broadcasted_iota(jnp.int32, (rows, block), 0) < live
    for j in range(masked_blocks.shape[0]):
        part = grad_ref[:, j * block : (j + 1) * block]
        masked_blocks[j] = jnp.where(alive, part, jnp.zeros_like(part))
    row_z(1).start()
    for h in range(2):
        rows_all[0, tensor, h] = masked_blocks[z * 2 + h]
    row_x(0).start()
    row_core(0).start()

    domain = domain_ref[dp]
    up_all[tensor, :rank] = dom_up_ref[domain]
    up_all[tensor, rank:] = com_up_ref[...]
    down_map[:rank] = dom_down_ref[domain]
    down_map[rank:] = com_down_ref[...]
    low_send[...] = jnp.zeros_like(low_send)
    back_all[tensor] = jnp.zeros_like(back_all.at[0])
    for j in range(n_tensor):
        low_send[j, :, :ranks] = nt_dot(act_ref[j * rows : (j + 1) * rows, :], down_map[...])

    row_z(1).wait_send()
    row_z(3).start()
    row_z(1).wait_recv()
    row_x(1).start()
    row_core(1).start()
    for m in range(1, n_tensor):
        up_copy(m).start()
        low_copy(m).start()
    row_x(0).wait_recv()
    row_forward(0).start()
    proj_copy(AHEAD - 1).start()
    finish_rows(1)

    take_proj(0)
    send_partial(0, 0)
    row_z(3).wait_send()
    row_z(2).start()
    take_proj(1)
    send_partial(0, 1)

    row_z(3).wait_recv()
    row_x(3).start()
    row_core(3).start()

    for m in range(1, n_tensor):
        up_copy(m).wait_recv()
    back = jnp.zeros((rows, ranks), jnp.float32)
    for j in range(masked_blocks.shape[0]):
        at = (j % per_tensor) * block
        back += nt_dot(masked_blocks[j], up_all[j // per_tensor, :, at : at + block])
    back_all[tensor, :, :ranks] = back.astype(jnp.bfloat16)
    for m in range(1, n_tensor):
        back_copy(m).start()

    low = low_send[tensor]
    for m in range(1, n_tensor):
        low_copy(m).wait_recv()
        low += low_recv[m - 1]
    low_flip = low.astype(jnp.bfloat16).astype(jnp.float32).T.astype(jnp.bfloat16)
    for j in range(masked_blocks.shape[0]):
        at = (j % per_tensor) * block
        part = adapter_scale * jnp.dot(
            low_flip, masked_blocks[j], preferred_element_type=jnp.float32
        )
        upg_send[j // per_tensor, :, at : at + block] = part[:ranks]

    finish_rows(3)
    send_partial(1, 0)
    send_partial(1, 1)
    take_proj(2)
    send_partial(0, 2)
    send_partial(1, 2)
    row_z(2).wait_recv()
    row_x(2).start()
    row_core(2).start()
    take_proj(3)
    send_partial(0, 3)
    send_partial(1, 3)
    finish_rows(2)
    for m in range(1, n_tensor):
        upg_copy(m).start()
    row_core(0).wait_recv()
    row_forward(0).wait_recv()
    early = 4

    lanes = back_all.shape[2]

    def send_sums():
        for m in range(1, n_tensor):
            back_copy(m).wait_recv()
        back_rows = back_all[...].reshape(series_rows, lanes)
        back_flip = back_rows.astype(jnp.float32).T.astype(jnp.bfloat16)
        for j in range(n_dp):
            at = slice(j * piece, (j + 1) * piece)
            part = adapter_scale * jnp.dot(
                back_flip, act_ref[:, at], preferred_element_type=jnp.float32
            )
            sum_send[j, :ranks] = part[:ranks].astype(jnp.bfloat16)
        for m in range(1, n_tensor):
            upg_copy(m).wait_recv()
        for j in range(n_dp):
            at = slice(j * piece, (j + 1) * piece)
            part = upg_send[tensor, :, at]
            for m in range(1, n_tensor):
                part += upg_recv[m - 1, :, at]
            sum_send[j, ranks:] = part.astype(jnp.bfloat16)
        for m in range(1, n_dp):
            sum_copy(m).start()
        sum_recv[dp] = sum_send[dp]

    def add_totals():
        for m in range(1, n_dp):
            sum_copy(m).wait_recv()
        for kind in range(2):
            base = kind * ranks
            to = kind * (domains * rank + srank)
            shared = jnp.zeros((srank, piece), jnp.float32)
            for r in range(n_dp):
                shared += sum_recv[r, base + rank : base + ranks].astype(jnp.float32)
            for k in range(domains):
                total = jnp.zeros((rank, piece), jnp.float32)
                for r in range(n_dp):
                    term = sum_recv[r, base : base + rank].astype(jnp.float32)
                    total += jnp.where(domain_ref[r] == k, term, jnp.zeros_like(term))
                total_all[dp, to + k * rank : to + (k + 1) * rank] = total.astype(jnp.bfloat16)
            to += domains * rank
            total_all[dp, to : to + srank] = shared.astype(jnp.bfloat16)

    def write_totals():
        side = domains * rank + srank
        for p in range(n_dp):
            at = slice(p * piece, (p + 1) * piece)
            for kind, dom_out, com_out in ((0, down_grad_ref, sdown_ref), (1, up_grad_ref, sup_ref)):
                for k in range(domains):
                    first = kind * side + k * rank
                    dom_out[k, :, at] = total_all[p, first : first + rank].astype(jnp.float32)
                first = kind * side + domains * rank
                com_out[:, at] = total_all[p, first : first + srank].astype(jnp.float32)

    @pl.loop(0, chunks + 2)
    def _(c):
        @pl.when(c + early < chunks)
        def _():
            take_proj(c + early)
            send_partial(0, c + early)
            send_partial(1, c + early)

        @pl.when(c < chunks)
        def _():
            kept[c, 1] = partial(2, c)
            kept[c, 0] = partial(0, c)

        @pl.when(jnp.logical_and(c >= 1, c <= chunks))
        def _():
            b = c - 1
            zl_copy(1, b).wait_recv()
            zh_send[b] = (kept[b, 1] + zl_recv[b, 1].astype(jnp.float32)).astype(jnp.bfloat16)
            zh_copy(b).start()

        @pl.when(c >= 2)
        def _():
            a = c - 2
            at = pl.ds(pl.multiple_of(a * CHUNK, CHUNK), CHUNK)
            adapter = jnp.dot(
                back_all[...].reshape(series_rows, lanes)[:, :ranks],
                down_map[:, at],
                preferred_element_type=jnp.float32,
            )
            zl_copy(0, a).wait_recv()
            whole = kept[a, 0] + zl_recv[a, 0].astype(jnp.float32) + adapter_scale * adapter
            zh_copy(a).wait_recv()
            out_ref[:, at] = (whole + zh_recv[a].astype(jnp.float32)).astype(jnp.bfloat16)

        @pl.when(c == 1)
        def _():
            send_sums()

        @pl.when(c == 3)
        def _():
            add_totals()
            total_copy(0, 4).start()

        @pl.when(c == 4)
        def _():
            total_copy(0, 4).wait_recv()
            for held in (0, 4):
                total_copy(held, 2).start()

        @pl.when(c == 5)
        def _():
            for held in (0, 4):
                total_copy(held, 2).wait_recv()
            for held in (0, 2, 4, 6):
                total_copy(held, 1).start()

        @pl.when(c == chunks)
        def _():
            for held in (0, 2, 4, 6):
                total_copy(held, 1).wait_recv()
            write_totals()

    @pl.loop(0, chunks)
    def _(c):
        zl_copy(0, c).wait_send()
        zl_copy(1, c).wait_send()
        zh_copy(c).wait_send()

    row_z(2).wait_send()
    for m in range(n_tensor):
        row_x(m).wait_send()
        row_core(m).wait_send()
        row_forward(m).wait_send()
    for m in range(1, n_tensor):
        up_copy(m).wait_send()
        low_copy(m).wait_send()
        back_copy(m).wait_send()
        upg_copy(m).wait_send()
    for m in range(1, n_dp):
        sum_copy(m).wait_send()
    for bit, helds in ((4, (0,)), (2, (0, 4)), (1, (0, 2, 4, 6))):
        for held in helds:
            total_copy(held, bit).wait_send()


def on_cube(
    n_dp,
    n_tensor,
    output_gradient,
    attention_output,
    frozen_projection,
    domain_down_map,
    domain_up_map,
    common_down_map,
    common_up_map,
    live_token_count,
    series_domain,
):
    rows, model = output_gradient.shape
    series_rows, width = attention_output.shape
    block = frozen_projection.shape[1]
    domains, rank = domain_down_map.shape[:2]
    srank = common_down_map.shape[0]
    ranks, side = rank + srank, domains * rank + srank
    chunks, piece, blocks = width // CHUNK, width // n_dp, model // block
    lanes = 128
    bf16, f32 = jnp.bfloat16, jnp.float32
    vmem = pl.BlockSpec(memory_space=pltpu.VMEM)
    smem = pl.BlockSpec(memory_space=pltpu.SMEM)

    def sems(count):
        return pltpu.SemaphoreType.DMA((2, count))

    return pl.pallas_call(
        functools.partial(cube_kernel, (n_dp, n_tensor, chunks)),
        out_shape=(
            jax.ShapeDtypeStruct((series_rows, width), bf16),
            jax.ShapeDtypeStruct((domains, rank, width), f32),
            jax.ShapeDtypeStruct((domains, rank, width), f32),
            jax.ShapeDtypeStruct((srank, width), f32),
            jax.ShapeDtypeStruct((srank, width), f32),
        ),
        in_specs=[smem] * 2 + [vmem] * 7,
        out_specs=(vmem,) * 5,
        scratch_shapes=[
            pltpu.VMEM((width, block), bf16),
            pltpu.VMEM((blocks, rows, block), bf16),
            pltpu.VMEM((4, n_tensor, 2, rows, block), bf16),
            pltpu.VMEM((n_tensor, ranks, width), bf16),
            pltpu.VMEM((ranks, width), bf16),
            pltpu.VMEM((n_tensor, rows, lanes), f32),
            pltpu.VMEM((n_tensor - 1, rows, lanes), f32),
            pltpu.VMEM((n_tensor, rows, lanes), bf16),
            pltpu.VMEM((n_tensor, ranks, width), f32),
            pltpu.VMEM((n_tensor - 1, ranks, width), f32),
            pltpu.VMEM((n_dp, 2 * ranks, piece), bf16),
            pltpu.VMEM((n_dp, 2 * ranks, piece), bf16),
            pltpu.VMEM((n_dp, 2 * side, piece), bf16),
            pltpu.VMEM((chunks, 2, series_rows, CHUNK), bf16),
            pltpu.VMEM((chunks, 2, series_rows, CHUNK), bf16),
            pltpu.VMEM((chunks, 2, series_rows, CHUNK), f32),
            pltpu.VMEM((chunks, series_rows, CHUNK), bf16),
            pltpu.VMEM((chunks, series_rows, CHUNK), bf16),
            sems(chunks),
            sems(3),
            sems(n_tensor),
            sems(n_tensor),
            sems(n_tensor),
            sems(n_tensor - 1),
            sems(n_tensor - 1),
            sems(n_tensor - 1),
            sems(n_tensor - 1),
            sems(n_dp - 1),
            sems(n_dp - 1),
            sems(2 * chunks),
            sems(chunks),
        ],
        compiler_params=pltpu.CompilerParams(
            collective_id=0, has_side_effects=True, vmem_limit_bytes=60 * 1024 * 1024
        ),
    )(
        live_token_count,
        series_domain,
        output_gradient,
        attention_output,
        frozen_projection,
        domain_down_map,
        domain_up_map,
        common_down_map,
        common_up_map,
    )


def solution(mesh):
    placed = (
        P(("dp", "tensor"), None),
        P("dp", "tensor"),
        P("tensor", "dp"),
        P(None, None, "tensor"),
        P(None, None, "tensor"),
        P(None, "tensor"),
        P(None, "tensor"),
        P("dp"),
        P(),
    )
    n_dp, n_tensor = mesh.shape["dp"], mesh.shape["tensor"]
    on_one = on_device
    if n_dp == 2**3 and n_tensor == 2**2:
        on_one = functools.partial(on_cube, n_dp, n_tensor)
    return jax.shard_map(
        on_one,
        mesh=mesh,
        in_specs=placed,
        out_specs=(
            P("dp", "tensor"),
            P(None, None, "tensor"),
            P(None, None, "tensor"),
            P(None, "tensor"),
            P(None, "tensor"),
        ),
        check_vma=False,
    )
```

```python
import functools

import jax
import jax.numpy as jnp
from jax import lax
from jax.experimental import pallas as pl
from jax.experimental.pallas import tpu as pltpu
from jax.sharding import PartitionSpec as P

adapter_scale = 2.0
shared_scale = 2.0
contract_dims = (((1,), (1,)), ((), ()))
outer_dims = (((0,), (0,)), ((), ()))


def on_device(
    output_gradient,
    attention_output,
    frozen_projection,
    domain_down_map,
    domain_up_map,
    common_down_map,
    common_up_map,
    live_token_count,
    series_domain,
):
    rows_local = output_gradient.shape[0]
    tensor_index = lax.axis_index("tensor")
    rank_index = lax.axis_index("dp")
    domain_number = lax.dynamic_index_in_dim(series_domain, rank_index, 0, keepdims=False)
    local_down_map = lax.dynamic_index_in_dim(domain_down_map, domain_number, 0, keepdims=False)
    local_up_map = lax.dynamic_index_in_dim(domain_up_map, domain_number, 0, keepdims=False)
    positions = tensor_index * rows_local + lax.iota(jnp.int32, rows_local)
    live_rows = (positions < live_token_count[0])[:, None]
    masked = jnp.where(live_rows, output_gradient, jnp.zeros_like(output_gradient))
    down_part = lax.dot_general(
        attention_output, local_down_map, contract_dims, preferred_element_type=jnp.float32
    )
    shared_part = lax.dot_general(
        attention_output, common_down_map, contract_dims, preferred_element_type=jnp.float32
    )
    down_total, shared_total = lax.psum((down_part, shared_part), "tensor")
    reduced_activation = down_total.astype(jnp.bfloat16)
    low_shared = shared_total.astype(jnp.bfloat16)
    gathered = lax.all_gather(masked, "tensor", axis=0, tiled=True)
    column_width = local_up_map.shape[1]
    my_columns = lax.dynamic_slice_in_dim(gathered, tensor_index * column_width, column_width, 1)
    dom_partial = lax.dot_general(
        my_columns, local_up_map, contract_dims, preferred_element_type=jnp.float32
    )
    shared_partial = lax.dot_general(
        my_columns, common_up_map, contract_dims, preferred_element_type=jnp.float32
    )
    dom_total, shared_back_total = lax.psum((dom_partial, shared_partial), "tensor")
    domain_backward = dom_total.astype(jnp.bfloat16)
    back_shared = shared_back_total.astype(jnp.bfloat16)
    local_down_gradient = adapter_scale * lax.dot_general(
        domain_backward, attention_output, outer_dims, preferred_element_type=jnp.float32
    )
    local_up_gradient = adapter_scale * lax.dot_general(
        reduced_activation, my_columns, outer_dims, preferred_element_type=jnp.float32
    )
    grad_sdown = shared_scale * lax.dot_general(
        back_shared, attention_output, outer_dims, preferred_element_type=jnp.float32
    )
    grad_sup = shared_scale * lax.dot_general(
        low_shared, my_columns, outer_dims, preferred_element_type=jnp.float32
    )
    domain_picker = (lax.iota(jnp.int32, domain_down_map.shape[0]) == domain_number).astype(
        jnp.float32
    )[:, None, None]
    frozen_total = lax.dot_general(
        gathered,
        lax.all_gather(frozen_projection, "dp", axis=1, tiled=True),
        contract_dims,
        preferred_element_type=jnp.float32,
    )
    summed = lax.psum(
        (
            domain_picker * local_down_gradient[None],
            domain_picker * local_up_gradient[None],
            grad_sdown,
            grad_sup,
        ),
        "dp",
    )
    adapter_contribution = adapter_scale * jnp.dot(
        domain_backward, local_down_map, preferred_element_type=jnp.float32
    )
    adapter_contribution = adapter_contribution + shared_scale * jnp.dot(
        back_shared, common_down_map, preferred_element_type=jnp.float32
    )
    grad_input = (frozen_total + adapter_contribution).astype(jnp.bfloat16)
    return (grad_input, summed[0], summed[1], summed[2], summed[3])

MESH = pl.DeviceIdType.MESH
CHUNK = 256
AHEAD = 3


def nt_dot(left, right):
    return lax.dot_general(left, right, contract_dims, preferred_element_type=jnp.float32)


def cube_kernel(
    dims,
    live_ref,
    domain_ref,
    grad_ref,
    act_ref,
    proj_ref,
    dom_down_ref,
    dom_up_ref,
    com_down_ref,
    com_up_ref,
    out_ref,
    adapters_ref,
    proj_mine,
    proj_other,
    masked_blocks,
    rows_all,
    up_all,
    down_map,
    low_send,
    low_recv,
    back_all,
    upg_send,
    upg_recv,
    sum_send,
    sum_recv,
    total_all,
    zl_send,
    zl_recv,
    zh_send,
    zh_recv,
    mine_sem,
    proj_sems,
    rowz_sems,
    rowx_sems,
    rowc_sems,
    rowf_sems,
    up_sems,
    low_sems,
    back_sems,
    upg_sems,
    sum_sems,
    total_sems,
    zl_sems,
    zh_sems,
):
    n_dp, n_tensor, chunks = dims
    dp = lax.axis_index("dp")
    tensor = lax.axis_index("tensor")
    y = lax.rem(dp, 2)
    z = dp // 2
    rows, block = masked_blocks.shape[1], masked_blocks.shape[2]
    series_rows = rows * n_tensor
    rank, srank = dom_down_ref.shape[1], com_down_ref.shape[0]
    ranks = rank + srank
    domains = dom_down_ref.shape[0]
    width = act_ref.shape[1]
    per_tensor = width // block
    piece = width // n_dp

    def flip(index, bit):
        return index + bit - 2 * bit * lax.rem(index // bit, 2)

    def flips(index, mask):
        for bit in (1, 2, 4):
            if mask & bit:
                index = flip(index, bit)
        return index

    def copy(src, dst, sems, at, dp_to, tensor_to):
        return pltpu.make_async_remote_copy(
            src_ref=src,
            dst_ref=dst,
            send_sem=sems.at[0, at],
            recv_sem=sems.at[1, at],
            device_id=(dp_to, tensor_to),
            device_id_type=MESH,
        )

    barrier = pltpu.get_barrier_semaphore()
    for mask in range(1, n_dp):
        pl.semaphore_signal(barrier, inc=1, device_id=(flips(dp, mask), tensor), device_id_type=MESH)
    for mask in range(1, n_tensor):
        pl.semaphore_signal(barrier, inc=1, device_id=(dp, flips(tensor, mask)), device_id_type=MESH)
    pl.semaphore_wait(barrier, n_dp + n_tensor - 2)

    def proj_copy(c):
        at = pl.ds(pl.multiple_of(c * CHUNK, CHUNK), CHUNK)
        return copy(proj_ref.at[at], proj_other.at[at], proj_sems, c, flip(dp, 1), tensor)

    def row_z(m):
        zt = flips(z, m)
        return copy(
            masked_blocks.at[pl.ds(zt * 2, 2)],
            rows_all.at[m, tensor],
            rowz_sems,
            m - 1,
            zt * 2 + y,
            tensor,
        )

    def row_x(m):
        here = rows_all.at[m, tensor]
        return copy(here, here, rowx_sems, m, dp, flip(tensor, 2))

    def row_core(m):
        here = rows_all.at[m, tensor]
        return copy(here, here, rowc_sems, m, dp, flip(tensor, 1))

    def row_forward(m):
        here = rows_all.at[m, flip(tensor, 2)]
        return copy(here, here, rowf_sems, m, dp, flip(tensor, 1))

    def up_copy(m):
        here = up_all.at[tensor]
        return copy(here, here, up_sems, m - 1, dp, flips(tensor, m))

    def low_copy(m):
        to = flips(tensor, m)
        return copy(low_send.at[to], low_recv.at[m - 1], low_sems, m - 1, dp, to)

    def back_copy(m):
        here = back_all.at[tensor]
        return copy(here, here, back_sems, m - 1, dp, flips(tensor, m))

    def upg_copy(m):
        to = flips(tensor, m)
        return copy(upg_send.at[to], upg_recv.at[m - 1], upg_sems, m - 1, dp, to)

    def sum_copy(m):
        to = flips(dp, m)
        return copy(sum_send.at[to], sum_recv.at[dp], sum_sems, m - 1, to, tensor)

    def total_copy(held, bit):
        here = total_all.at[flips(dp, held)]
        return copy(here, here, total_sems, (held | bit) - 1, flip(dp, bit), tensor)

    def zl_copy(k, c):
        part_of = zl_send.at[c, k]
        return copy(part_of, zl_recv.at[c, k], zl_sems, 2 * c + k, flip(z, 1) * 2 + y, tensor)

    def zh_copy(c):
        return copy(zh_send.at[c], zh_recv.at[c], zh_sems, c, flip(z, 2) * 2 + y, tensor)

    def partial(m, c):
        at = pl.ds(pl.multiple_of(c * CHUNK, CHUNK), CHUNK)
        own = rows_all[m, :, y].reshape(series_rows, block)
        other = rows_all[m, :, 1 - y].reshape(series_rows, block)
        return nt_dot(own, proj_mine[at, :]) + nt_dot(other, proj_other[at, :])

    def take_proj(c):
        proj_copy(c).wait_recv()

        proj_copy(c).wait_send()

        @pl.when(c + AHEAD < chunks)
        def _():
            proj_copy(c + AHEAD).start()

    def send_partial(k, c):
        zl_send[c, k] = partial(2 * k + 1, c).astype(jnp.bfloat16)
        zl_copy(k, c).start()

    def finish_rows(m):
        row_x(m).wait_recv()
        row_forward(m).start()
        row_core(m).wait_recv()
        row_forward(m).wait_recv()

    for c in range(AHEAD - 1):
        proj_copy(c).start()
    mine = pltpu.make_async_copy(proj_ref, proj_mine, mine_sem)
    mine.start()

    live = live_ref[0]
    alive = tensor * rows + lax.broadcasted_iota(jnp.int32, (rows, block), 0) < live
    for j in range(masked_blocks.shape[0]):
        part = grad_ref[:, j * block : (j + 1) * block]
        masked_blocks[j] = jnp.where(alive, part, jnp.zeros_like(part))
    row_z(1).start()
    for h in range(2):
        rows_all[0, tensor, h] = masked_blocks[z * 2 + h]

    domain = domain_ref[dp]
    up_all[tensor, :rank] = dom_up_ref[domain]
    up_all[tensor, rank:] = com_up_ref[...]
    for m in range(1, n_tensor):
        up_copy(m).start()
    down_map[:rank] = dom_down_ref[domain]
    down_map[rank:] = com_down_ref[...]
    low_send[...] = jnp.zeros_like(low_send)
    back_all[tensor] = jnp.zeros_like(back_all.at[0])
    for j in range(n_tensor):
        low_send[j, :, :ranks] = nt_dot(act_ref[j * rows : (j + 1) * rows, :], down_map[...])
    for m in range(1, n_tensor):
        low_copy(m).start()

    row_z(1).wait_send()
    row_z(3).start()
    row_z(1).wait_recv()
    row_x(1).start()
    row_core(1).start()
    proj_copy(AHEAD - 1).start()
    finish_rows(1)
    row_x(0).start()
    row_core(0).start()

    mine.wait()
    take_proj(0)
    send_partial(0, 0)
    take_proj(1)
    send_partial(0, 1)
    row_z(3).wait_send()
    row_z(2).start()

    row_z(3).wait_recv()
    row_x(3).start()
    row_core(3).start()

    for m in range(1, n_tensor):
        up_copy(m).wait_recv()
    back = jnp.zeros((rows, ranks), jnp.float32)
    for j in range(masked_blocks.shape[0]):
        at = (j % per_tensor) * block
        back += nt_dot(masked_blocks[j], up_all[j // per_tensor, :, at : at + block])
    back_all[tensor, :, :ranks] = back.astype(jnp.bfloat16)
    for m in range(1, n_tensor):
        back_copy(m).start()

    low = low_send[tensor]
    for m in range(1, n_tensor):
        low_copy(m).wait_recv()
        low += low_recv[m - 1]
    low_flip = low.astype(jnp.bfloat16).astype(jnp.float32).T.astype(jnp.bfloat16)
    for j in range(masked_blocks.shape[0]):
        at = (j % per_tensor) * block
        part = adapter_scale * jnp.dot(
            low_flip, masked_blocks[j], preferred_element_type=jnp.float32
        )
        upg_send[j // per_tensor, :, at : at + block] = part[:ranks].astype(jnp.bfloat16)

    for m in range(1, n_tensor):
        upg_copy(m).start()
    finish_rows(3)
    send_partial(1, 0)
    send_partial(1, 1)
    take_proj(2)
    send_partial(0, 2)
    send_partial(1, 2)
    row_z(2).wait_recv()
    row_x(2).start()
    row_core(2).start()
    take_proj(3)
    send_partial(0, 3)
    send_partial(1, 3)
    finish_rows(2)
    finish_rows(0)
    early = 4

    lanes = back_all.shape[2]

    def send_sums():
        for m in range(1, n_tensor):
            back_copy(m).wait_recv()
        back_rows = back_all[...].reshape(series_rows, lanes)
        back_flip = back_rows.astype(jnp.float32).T.astype(jnp.bfloat16)
        for j in range(n_dp):
            at = slice(j * piece, (j + 1) * piece)
            part = adapter_scale * jnp.dot(
                back_flip, act_ref[:, at], preferred_element_type=jnp.float32
            )
            sum_send[j, :ranks] = part[:ranks].astype(jnp.bfloat16)
        for m in range(1, n_tensor):
            upg_copy(m).wait_recv()
        for j in range(n_dp):
            at = slice(j * piece, (j + 1) * piece)
            part = upg_send[tensor, :, at].astype(jnp.float32)
            for m in range(1, n_tensor):
                part += upg_recv[m - 1, :, at].astype(jnp.float32)
            sum_send[j, ranks:] = part.astype(jnp.bfloat16)
        for m in range(1, n_dp):
            sum_copy(m).start()
        sum_recv[dp] = sum_send[dp]

    def add_totals():
        for m in range(1, n_dp):
            sum_copy(m).wait_recv()
        for kind in range(2):
            base = kind * ranks
            to = kind * (domains * rank + srank)
            shared = jnp.zeros((srank, piece), jnp.float32)
            for r in range(n_dp):
                shared += sum_recv[r, base + rank : base + ranks].astype(jnp.float32)
            for k in range(domains):
                total = jnp.zeros((rank, piece), jnp.float32)
                for r in range(n_dp):
                    term = sum_recv[r, base : base + rank].astype(jnp.float32)
                    total += jnp.where(domain_ref[r] == k, term, jnp.zeros_like(term))
                total_all[dp, to + k * rank : to + (k + 1) * rank] = total.astype(jnp.bfloat16)
            to += domains * rank
            total_all[dp, to : to + srank] = shared.astype(jnp.bfloat16)

    def write_totals():
        for p in range(n_dp):
            adapters_ref[:, p * piece : (p + 1) * piece] = total_all[p]

    @pl.loop(0, chunks + 2)
    def _(c):
        @pl.when(c < chunks)
        def _():
            own = partial(2, c)
            zl_copy(1, c).wait_recv()
            zh_send[c] = (own + zl_recv[c, 1].astype(jnp.float32)).astype(jnp.bfloat16)
            zh_copy(c).start()

        @pl.when(c + early < chunks)
        def _():
            take_proj(c + early)
            send_partial(0, c + early)
            send_partial(1, c + early)

        @pl.when(c >= 2)
        def _():
            a = c - 2
            at = pl.ds(pl.multiple_of(a * CHUNK, CHUNK), CHUNK)
            adapter = jnp.dot(
                back_all[...].reshape(series_rows, lanes)[:, :ranks],
                down_map[:, at],
                preferred_element_type=jnp.float32,
            )
            whole = partial(0, a) + adapter_scale * adapter
            zl_copy(0, a).wait_recv()
            zh_copy(a).wait_recv()
            whole += zl_recv[a, 0].astype(jnp.float32)
            out_ref[:, at] = (whole + zh_recv[a].astype(jnp.float32)).astype(jnp.bfloat16)

        @pl.when(c == 1)
        def _():
            send_sums()

        @pl.when(c == 3)
        def _():
            add_totals()
            total_copy(0, 4).start()

        @pl.when(c == 5)
        def _():
            total_copy(0, 4).wait_recv()
            for held in (0, 4):
                total_copy(held, 2).start()

        @pl.when(c == 6)
        def _():
            for held in (0, 4):
                total_copy(held, 2).wait_recv()
            for held in (0, 2, 4, 6):
                total_copy(held, 1).start()

        @pl.when(c == chunks)
        def _():
            for held in (0, 2, 4, 6):
                total_copy(held, 1).wait_recv()
            write_totals()

    @pl.loop(0, chunks)
    def _(c):
        zl_copy(0, c).wait_send()
        zl_copy(1, c).wait_send()
        zh_copy(c).wait_send()

    row_z(2).wait_send()
    for m in range(n_tensor):
        row_x(m).wait_send()
        row_core(m).wait_send()
        row_forward(m).wait_send()
    for m in range(1, n_tensor):
        up_copy(m).wait_send()
        low_copy(m).wait_send()
        back_copy(m).wait_send()
        upg_copy(m).wait_send()
    for m in range(1, n_dp):
        sum_copy(m).wait_send()
    for bit, helds in ((4, (0,)), (2, (0, 4)), (1, (0, 2, 4, 6))):
        for held in helds:
            total_copy(held, bit).wait_send()


def on_cube(
    n_dp,
    n_tensor,
    output_gradient,
    attention_output,
    frozen_projection,
    domain_down_map,
    domain_up_map,
    common_down_map,
    common_up_map,
    live_token_count,
    series_domain,
):
    rows, model = output_gradient.shape
    series_rows, width = attention_output.shape
    block = frozen_projection.shape[1]
    domains, rank = domain_down_map.shape[:2]
    srank = common_down_map.shape[0]
    ranks, side = rank + srank, domains * rank + srank
    chunks, piece, blocks = width // CHUNK, width // n_dp, model // block
    lanes = 128
    bf16, f32 = jnp.bfloat16, jnp.float32
    vmem = pl.BlockSpec(memory_space=pltpu.VMEM)
    smem = pl.BlockSpec(memory_space=pltpu.SMEM)

    def sems(count):
        return pltpu.SemaphoreType.DMA((2, count))

    grad_input, adapters = pl.pallas_call(
        functools.partial(cube_kernel, (n_dp, n_tensor, chunks)),
        out_shape=(
            jax.ShapeDtypeStruct((series_rows, width), bf16),
            jax.ShapeDtypeStruct((2 * side, width), bf16),
        ),
        in_specs=[smem] * 2 + [vmem] * 2 + [pl.BlockSpec(memory_space=pl.ANY)] + [vmem] * 4,
        out_specs=(vmem,) * 2,
        scratch_shapes=[
            pltpu.VMEM((width, block), bf16),
            pltpu.VMEM((width, block), bf16),
            pltpu.VMEM((blocks, rows, block), bf16),
            pltpu.VMEM((4, n_tensor, 2, rows, block), bf16),
            pltpu.VMEM((n_tensor, ranks, width), bf16),
            pltpu.VMEM((ranks, width), bf16),
            pltpu.VMEM((n_tensor, rows, lanes), f32),
            pltpu.VMEM((n_tensor - 1, rows, lanes), f32),
            pltpu.VMEM((n_tensor, rows, lanes), bf16),
            pltpu.VMEM((n_tensor, ranks, width), bf16),
            pltpu.VMEM((n_tensor - 1, ranks, width), bf16),
            pltpu.VMEM((n_dp, 2 * ranks, piece), bf16),
            pltpu.VMEM((n_dp, 2 * ranks, piece), bf16),
            pltpu.VMEM((n_dp, 2 * side, piece), bf16),
            pltpu.VMEM((chunks, 2, series_rows, CHUNK), bf16),
            pltpu.VMEM((chunks, 2, series_rows, CHUNK), bf16),
            pltpu.VMEM((chunks, series_rows, CHUNK), bf16),
            pltpu.VMEM((chunks, series_rows, CHUNK), bf16),
            pltpu.SemaphoreType.DMA,
            sems(chunks),
            sems(3),
            sems(n_tensor),
            sems(n_tensor),
            sems(n_tensor),
            sems(n_tensor - 1),
            sems(n_tensor - 1),
            sems(n_tensor - 1),
            sems(n_tensor - 1),
            sems(n_dp - 1),
            sems(n_dp - 1),
            sems(2 * chunks),
            sems(chunks),
        ],
        compiler_params=pltpu.CompilerParams(
            collective_id=0, has_side_effects=True, vmem_limit_bytes=60 * 1024 * 1024
        ),
    )(
        live_token_count,
        series_domain,
        output_gradient,
        attention_output,
        frozen_projection,
        domain_down_map,
        domain_up_map,
        common_down_map,
        common_up_map,
    )
    split = domains * rank
    adapters = adapters.astype(f32)
    return (
        grad_input,
        adapters[:split].reshape(domains, rank, width),
        adapters[side : side + split].reshape(domains, rank, width),
        adapters[split:side],
        adapters[side + split :],
    )


def solution(mesh):
    placed = (
        P(("dp", "tensor"), None),
        P("dp", "tensor"),
        P("tensor", "dp"),
        P(None, None, "tensor"),
        P(None, None, "tensor"),
        P(None, "tensor"),
        P(None, "tensor"),
        P("dp"),
        P(),
    )
    n_dp, n_tensor = mesh.shape["dp"], mesh.shape["tensor"]
    on_one = on_device
    if n_dp == 2**3 and n_tensor == 2**2:
        on_one = functools.partial(on_cube, n_dp, n_tensor)
    return jax.shard_map(
        on_one,
        mesh=mesh,
        in_specs=placed,
        out_specs=(
            P("dp", "tensor"),
            P(None, None, "tensor"),
            P(None, None, "tensor"),
            P(None, "tensor"),
            P(None, "tensor"),
        ),
        check_vma=False,
    )
```

```python
import functools

import jax
import jax.numpy as jnp
from jax import lax
from jax.experimental import pallas as pl
from jax.experimental.pallas import tpu as pltpu
from jax.sharding import PartitionSpec as P

adapter_scale = 2.0
shared_scale = 2.0
contract_dims = (((1,), (1,)), ((), ()))
outer_dims = (((0,), (0,)), ((), ()))


def on_device(
    output_gradient,
    attention_output,
    frozen_projection,
    domain_down_map,
    domain_up_map,
    common_down_map,
    common_up_map,
    live_token_count,
    series_domain,
):
    rows_local = output_gradient.shape[0]
    tensor_index = lax.axis_index("tensor")
    rank_index = lax.axis_index("dp")
    domain_number = lax.dynamic_index_in_dim(series_domain, rank_index, 0, keepdims=False)
    local_down_map = lax.dynamic_index_in_dim(domain_down_map, domain_number, 0, keepdims=False)
    local_up_map = lax.dynamic_index_in_dim(domain_up_map, domain_number, 0, keepdims=False)
    positions = tensor_index * rows_local + lax.iota(jnp.int32, rows_local)
    live_rows = (positions < live_token_count[0])[:, None]
    masked = jnp.where(live_rows, output_gradient, jnp.zeros_like(output_gradient))
    down_part = lax.dot_general(
        attention_output, local_down_map, contract_dims, preferred_element_type=jnp.float32
    )
    shared_part = lax.dot_general(
        attention_output, common_down_map, contract_dims, preferred_element_type=jnp.float32
    )
    down_total, shared_total = lax.psum((down_part, shared_part), "tensor")
    reduced_activation = down_total.astype(jnp.bfloat16)
    low_shared = shared_total.astype(jnp.bfloat16)
    gathered = lax.all_gather(masked, "tensor", axis=0, tiled=True)
    column_width = local_up_map.shape[1]
    my_columns = lax.dynamic_slice_in_dim(gathered, tensor_index * column_width, column_width, 1)
    dom_partial = lax.dot_general(
        my_columns, local_up_map, contract_dims, preferred_element_type=jnp.float32
    )
    shared_partial = lax.dot_general(
        my_columns, common_up_map, contract_dims, preferred_element_type=jnp.float32
    )
    dom_total, shared_back_total = lax.psum((dom_partial, shared_partial), "tensor")
    domain_backward = dom_total.astype(jnp.bfloat16)
    back_shared = shared_back_total.astype(jnp.bfloat16)
    local_down_gradient = adapter_scale * lax.dot_general(
        domain_backward, attention_output, outer_dims, preferred_element_type=jnp.float32
    )
    local_up_gradient = adapter_scale * lax.dot_general(
        reduced_activation, my_columns, outer_dims, preferred_element_type=jnp.float32
    )
    grad_sdown = shared_scale * lax.dot_general(
        back_shared, attention_output, outer_dims, preferred_element_type=jnp.float32
    )
    grad_sup = shared_scale * lax.dot_general(
        low_shared, my_columns, outer_dims, preferred_element_type=jnp.float32
    )
    domain_picker = (lax.iota(jnp.int32, domain_down_map.shape[0]) == domain_number).astype(
        jnp.float32
    )[:, None, None]
    frozen_total = lax.dot_general(
        gathered,
        lax.all_gather(frozen_projection, "dp", axis=1, tiled=True),
        contract_dims,
        preferred_element_type=jnp.float32,
    )
    summed = lax.psum(
        (
            domain_picker * local_down_gradient[None],
            domain_picker * local_up_gradient[None],
            grad_sdown,
            grad_sup,
        ),
        "dp",
    )
    adapter_contribution = adapter_scale * jnp.dot(
        domain_backward, local_down_map, preferred_element_type=jnp.float32
    )
    adapter_contribution = adapter_contribution + shared_scale * jnp.dot(
        back_shared, common_down_map, preferred_element_type=jnp.float32
    )
    grad_input = (frozen_total + adapter_contribution).astype(jnp.bfloat16)
    return (grad_input, summed[0], summed[1], summed[2], summed[3])

MESH = pl.DeviceIdType.MESH
CHUNK = 256
AHEAD = 3


def nt_dot(left, right):
    return lax.dot_general(left, right, contract_dims, preferred_element_type=jnp.float32)


def cube_kernel(
    dims,
    live_ref,
    domain_ref,
    grad_ref,
    act_ref,
    proj_ref,
    dom_down_ref,
    dom_up_ref,
    com_down_ref,
    com_up_ref,
    out_ref,
    adapters_ref,
    proj_mine,
    proj_other,
    masked_blocks,
    rows_all,
    up_all,
    down_map,
    low_send,
    low_recv,
    back_all,
    upg_send,
    upg_recv,
    sum_send,
    sum_recv,
    total_all,
    zl_send,
    zl_recv,
    zh_send,
    zh_recv,
    mine_sem,
    proj_sems,
    rowz_sems,
    rowx_sems,
    rowc_sems,
    rowf_sems,
    up_sems,
    low_sems,
    back_sems,
    upg_sems,
    sum_sems,
    total_sems,
    zl_sems,
    zh_sems,
):
    n_dp, n_tensor, chunks = dims
    dp = lax.axis_index("dp")
    tensor = lax.axis_index("tensor")
    y = lax.rem(dp, 2)
    z = dp // 2
    rows, block = masked_blocks.shape[1], masked_blocks.shape[2]
    series_rows = rows * n_tensor
    rank, srank = dom_down_ref.shape[1], com_down_ref.shape[0]
    ranks = rank + srank
    domains = dom_down_ref.shape[0]
    width = act_ref.shape[1]
    per_tensor = width // block
    piece = width // n_dp

    def flip(index, bit):
        return index + bit - 2 * bit * lax.rem(index // bit, 2)

    def flips(index, mask):
        for bit in (1, 2, 4):
            if mask & bit:
                index = flip(index, bit)
        return index

    def copy(src, dst, sems, at, dp_to, tensor_to):
        return pltpu.make_async_remote_copy(
            src_ref=src,
            dst_ref=dst,
            send_sem=sems.at[0, at],
            recv_sem=sems.at[1, at],
            device_id=(dp_to, tensor_to),
            device_id_type=MESH,
        )

    barrier = pltpu.get_barrier_semaphore()
    for mask in range(1, n_dp):
        pl.semaphore_signal(barrier, inc=1, device_id=(flips(dp, mask), tensor), device_id_type=MESH)
    for mask in range(1, n_tensor):
        pl.semaphore_signal(barrier, inc=1, device_id=(dp, flips(tensor, mask)), device_id_type=MESH)
    pl.semaphore_wait(barrier, n_dp + n_tensor - 2)

    def proj_copy(c):
        at = pl.ds(pl.multiple_of(c * CHUNK, CHUNK), CHUNK)
        return copy(proj_ref.at[at], proj_other.at[at], proj_sems, c, flip(dp, 1), tensor)

    def row_z(m, h):
        zt = flips(z, m)
        return copy(
            masked_blocks.at[zt * 2 + h],
            rows_all.at[m, tensor, h],
            rowz_sems,
            2 * (m - 1) + h,
            zt * 2 + y,
            tensor,
        )

    def row_x(m, h):
        here = rows_all.at[m, tensor, h]
        return copy(here, here, rowx_sems, 2 * m + h, dp, flip(tensor, 2))

    def row_core(m, h):
        here = rows_all.at[m, tensor, h]
        return copy(here, here, rowc_sems, 2 * m + h, dp, flip(tensor, 1))

    def row_forward(m, h):
        here = rows_all.at[m, flip(tensor, 2), h]
        return copy(here, here, rowf_sems, 2 * m + h, dp, flip(tensor, 1))

    def share_rows(m):
        for h in range(2):
            row_x(m, h).start()
            row_core(m, h).start()

    def up_copy(m):
        here = up_all.at[tensor]
        return copy(here, here, up_sems, m - 1, dp, flips(tensor, m))

    def low_copy(m):
        to = flips(tensor, m)
        return copy(low_send.at[to], low_recv.at[m - 1], low_sems, m - 1, dp, to)

    def back_copy(m):
        here = back_all.at[tensor]
        return copy(here, here, back_sems, m - 1, dp, flips(tensor, m))

    def upg_copy(m):
        to = flips(tensor, m)
        return copy(upg_send.at[to], upg_recv.at[m - 1], upg_sems, m - 1, dp, to)

    def sum_copy(m):
        to = flips(dp, m)
        return copy(sum_send.at[to], sum_recv.at[dp], sum_sems, m - 1, to, tensor)

    def total_copy(held, bit):
        here = total_all.at[flips(dp, held)]
        return copy(here, here, total_sems, (held | bit) - 1, flip(dp, bit), tensor)

    def zl_copy(k, c):
        part_of = zl_send.at[c, k]
        return copy(part_of, zl_recv.at[c, k], zl_sems, 2 * c + k, flip(z, 1) * 2 + y, tensor)

    def zh_copy(c):
        return copy(zh_send.at[c], zh_recv.at[c], zh_sems, c, flip(z, 2) * 2 + y, tensor)

    def partial(m, c):
        at = pl.ds(pl.multiple_of(c * CHUNK, CHUNK), CHUNK)
        own = rows_all[m, :, y].reshape(series_rows, block)
        other = rows_all[m, :, 1 - y].reshape(series_rows, block)
        return nt_dot(own, proj_mine[at, :]) + nt_dot(other, proj_other[at, :])

    def take_proj(c):
        proj_copy(c).wait_recv()

        proj_copy(c).wait_send()

        @pl.when(c + AHEAD < chunks)
        def _():
            proj_copy(c + AHEAD).start()

    def send_partial(k, c):
        zl_send[c, k] = partial(2 * k + 1, c).astype(jnp.bfloat16)
        zl_copy(k, c).start()

    def finish_rows(m):
        for h in range(2):
            row_x(m, h).wait_recv()
            row_forward(m, h).start()
        for h in range(2):
            row_core(m, h).wait_recv()
            row_forward(m, h).wait_recv()

    proj_copy(0).start()
    mine = pltpu.make_async_copy(proj_ref, proj_mine, mine_sem)
    mine.start()

    live = live_ref[0]
    alive = tensor * rows + lax.broadcasted_iota(jnp.int32, (rows, block), 0) < live
    for j in range(masked_blocks.shape[0]):
        part = grad_ref[:, j * block : (j + 1) * block]
        masked_blocks[j] = jnp.where(alive, part, jnp.zeros_like(part))
    row_z(1, 0).start()
    for h in range(2):
        rows_all[0, tensor, h] = masked_blocks[z * 2 + h]

    domain = domain_ref[dp]
    up_all[tensor, :rank] = dom_up_ref[domain]
    up_all[tensor, rank:] = com_up_ref[...]
    for m in range(1, n_tensor):
        up_copy(m).start()
    down_map[:rank] = dom_down_ref[domain]
    down_map[rank:] = com_down_ref[...]
    low_send[...] = jnp.zeros_like(low_send)
    back_all[tensor] = jnp.zeros_like(back_all.at[0])
    for j in range(n_tensor):
        low_send[j, :, :ranks] = nt_dot(act_ref[j * rows : (j + 1) * rows, :], down_map[...])
    for m in range(1, n_tensor):
        low_copy(m).start()

    row_z(1, 0).wait_send()
    row_z(1, 1).start()
    row_z(1, 0).wait_recv()
    row_x(1, 0).start()
    row_core(1, 0).start()
    row_z(1, 1).wait_send()
    for h in range(2):
        row_z(3, h).start()
    row_z(1, 1).wait_recv()
    row_x(1, 1).start()
    row_core(1, 1).start()
    proj_copy(1).start()
    finish_rows(1)
    share_rows(0)
    for c in range(2, AHEAD):
        proj_copy(c).start()

    mine.wait()
    take_proj(0)
    send_partial(0, 0)
    take_proj(1)
    send_partial(0, 1)
    for h in range(2):
        row_z(3, h).wait_send()
    for h in range(2):
        row_z(2, h).start()

    for h in range(2):
        row_z(3, h).wait_recv()
    share_rows(3)

    for m in range(1, n_tensor):
        up_copy(m).wait_recv()
    back = jnp.zeros((rows, ranks), jnp.float32)
    for j in range(masked_blocks.shape[0]):
        at = (j % per_tensor) * block
        back += nt_dot(masked_blocks[j], up_all[j // per_tensor, :, at : at + block])
    back_all[tensor, :, :ranks] = back.astype(jnp.bfloat16)
    for m in range(1, n_tensor):
        back_copy(m).start()

    low = low_send[tensor]
    for m in range(1, n_tensor):
        low_copy(m).wait_recv()
        low += low_recv[m - 1]
    low_flip = low.astype(jnp.bfloat16).astype(jnp.float32).T.astype(jnp.bfloat16)
    for j in range(masked_blocks.shape[0]):
        at = (j % per_tensor) * block
        part = adapter_scale * jnp.dot(
            low_flip, masked_blocks[j], preferred_element_type=jnp.float32
        )
        upg_send[j // per_tensor, :, at : at + block] = part[:ranks].astype(jnp.bfloat16)

    for m in range(1, n_tensor):
        upg_copy(m).start()
    finish_rows(3)
    send_partial(1, 0)
    send_partial(1, 1)
    take_proj(2)
    send_partial(0, 2)
    send_partial(1, 2)
    for h in range(2):
        row_z(2, h).wait_recv()
    share_rows(2)
    take_proj(3)
    send_partial(0, 3)
    send_partial(1, 3)
    finish_rows(2)
    finish_rows(0)
    early = 4

    lanes = back_all.shape[2]

    def send_sums():
        for m in range(1, n_tensor):
            back_copy(m).wait_recv()
        back_rows = back_all[...].reshape(series_rows, lanes)
        back_flip = back_rows.astype(jnp.float32).T.astype(jnp.bfloat16)
        for j in range(n_dp):
            at = slice(j * piece, (j + 1) * piece)
            part = adapter_scale * jnp.dot(
                back_flip, act_ref[:, at], preferred_element_type=jnp.float32
            )
            sum_send[j, :ranks] = part[:ranks].astype(jnp.bfloat16)
        for m in range(1, n_tensor):
            upg_copy(m).wait_recv()
        for j in range(n_dp):
            at = slice(j * piece, (j + 1) * piece)
            part = upg_send[tensor, :, at].astype(jnp.float32)
            for m in range(1, n_tensor):
                part += upg_recv[m - 1, :, at].astype(jnp.float32)
            sum_send[j, ranks:] = part.astype(jnp.bfloat16)
        for m in range(1, n_dp):
            sum_copy(m).start()
        sum_recv[dp] = sum_send[dp]

    def add_totals():
        for m in range(1, n_dp):
            sum_copy(m).wait_recv()
        for kind in range(2):
            base = kind * ranks
            to = kind * (domains * rank + srank)
            shared = jnp.zeros((srank, piece), jnp.float32)
            for r in range(n_dp):
                shared += sum_recv[r, base + rank : base + ranks].astype(jnp.float32)
            for k in range(domains):
                total = jnp.zeros((rank, piece), jnp.float32)
                for r in range(n_dp):
                    term = sum_recv[r, base : base + rank].astype(jnp.float32)
                    total += jnp.where(domain_ref[r] == k, term, jnp.zeros_like(term))
                total_all[dp, to + k * rank : to + (k + 1) * rank] = total.astype(jnp.bfloat16)
            to += domains * rank
            total_all[dp, to : to + srank] = shared.astype(jnp.bfloat16)

    def write_totals():
        for p in range(n_dp):
            adapters_ref[:, p * piece : (p + 1) * piece] = total_all[p]

    @pl.loop(0, chunks + 2)
    def _(c):
        @pl.when(c < chunks)
        def _():
            own = partial(2, c)
            zl_copy(1, c).wait_recv()
            zh_send[c] = (own + zl_recv[c, 1].astype(jnp.float32)).astype(jnp.bfloat16)
            zh_copy(c).start()

        @pl.when(c + early < chunks)
        def _():
            take_proj(c + early)
            send_partial(0, c + early)
            send_partial(1, c + early)

        @pl.when(c >= 2)
        def _():
            a = c - 2
            at = pl.ds(pl.multiple_of(a * CHUNK, CHUNK), CHUNK)
            adapter = jnp.dot(
                back_all[...].reshape(series_rows, lanes)[:, :ranks],
                down_map[:, at],
                preferred_element_type=jnp.float32,
            )
            whole = partial(0, a) + adapter_scale * adapter
            zl_copy(0, a).wait_recv()
            zh_copy(a).wait_recv()
            whole += zl_recv[a, 0].astype(jnp.float32)
            out_ref[:, at] = (whole + zh_recv[a].astype(jnp.float32)).astype(jnp.bfloat16)

        @pl.when(c == 1)
        def _():
            send_sums()

        @pl.when(c == 3)
        def _():
            add_totals()
            total_copy(0, 4).start()

        @pl.when(c == 5)
        def _():
            total_copy(0, 4).wait_recv()
            for held in (0, 4):
                total_copy(held, 2).start()

        @pl.when(c == 6)
        def _():
            for held in (0, 4):
                total_copy(held, 2).wait_recv()
            for held in (0, 2, 4, 6):
                total_copy(held, 1).start()

        @pl.when(c == chunks)
        def _():
            for held in (0, 2, 4, 6):
                total_copy(held, 1).wait_recv()
            write_totals()

    @pl.loop(0, chunks)
    def _(c):
        zl_copy(0, c).wait_send()
        zl_copy(1, c).wait_send()
        zh_copy(c).wait_send()

    for h in range(2):
        row_z(2, h).wait_send()
        for m in range(n_tensor):
            row_x(m, h).wait_send()
            row_core(m, h).wait_send()
            row_forward(m, h).wait_send()
    for m in range(1, n_tensor):
        up_copy(m).wait_send()
        low_copy(m).wait_send()
        back_copy(m).wait_send()
        upg_copy(m).wait_send()
    for m in range(1, n_dp):
        sum_copy(m).wait_send()
    for bit, helds in ((4, (0,)), (2, (0, 4)), (1, (0, 2, 4, 6))):
        for held in helds:
            total_copy(held, bit).wait_send()


def widen_kernel(grad_ref, sums_ref, grad_out, down_out, up_out, sdown_out, sup_out):
    grad_out[...] = grad_ref[...]
    domains, rank = down_out.shape[:2]
    first = 0
    for dom_out, com_out in ((down_out, sdown_out), (up_out, sup_out)):
        for k in range(domains):
            dom_out[k] = sums_ref[first : first + rank].astype(jnp.float32)
            first += rank
        com_out[...] = sums_ref[first : first + com_out.shape[0]].astype(jnp.float32)
        first += com_out.shape[0]


def on_cube(
    n_dp,
    n_tensor,
    output_gradient,
    attention_output,
    frozen_projection,
    domain_down_map,
    domain_up_map,
    common_down_map,
    common_up_map,
    live_token_count,
    series_domain,
):
    rows, model = output_gradient.shape
    series_rows, width = attention_output.shape
    block = frozen_projection.shape[1]
    domains, rank = domain_down_map.shape[:2]
    srank = common_down_map.shape[0]
    ranks, side = rank + srank, domains * rank + srank
    chunks, piece, blocks = width // CHUNK, width // n_dp, model // block
    lanes = 128
    bf16, f32 = jnp.bfloat16, jnp.float32
    vmem = pl.BlockSpec(memory_space=pltpu.VMEM)
    smem = pl.BlockSpec(memory_space=pltpu.SMEM)

    def sems(count):
        return pltpu.SemaphoreType.DMA((2, count))

    grad_input, adapters = pl.pallas_call(
        functools.partial(cube_kernel, (n_dp, n_tensor, chunks)),
        out_shape=(
            jax.ShapeDtypeStruct((series_rows, width), bf16),
            jax.ShapeDtypeStruct((2 * side, width), bf16),
        ),
        in_specs=[smem] * 2 + [vmem] * 2 + [pl.BlockSpec(memory_space=pl.ANY)] + [vmem] * 4,
        out_specs=(vmem,) * 2,
        scratch_shapes=[
            pltpu.VMEM((width, block), bf16),
            pltpu.VMEM((width, block), bf16),
            pltpu.VMEM((blocks, rows, block), bf16),
            pltpu.VMEM((4, n_tensor, 2, rows, block), bf16),
            pltpu.VMEM((n_tensor, ranks, width), bf16),
            pltpu.VMEM((ranks, width), bf16),
            pltpu.VMEM((n_tensor, rows, lanes), f32),
            pltpu.VMEM((n_tensor - 1, rows, lanes), f32),
            pltpu.VMEM((n_tensor, rows, lanes), bf16),
            pltpu.VMEM((n_tensor, ranks, width), bf16),
            pltpu.VMEM((n_tensor - 1, ranks, width), bf16),
            pltpu.VMEM((n_dp, 2 * ranks, piece), bf16),
            pltpu.VMEM((n_dp, 2 * ranks, piece), bf16),
            pltpu.VMEM((n_dp, 2 * side, piece), bf16),
            pltpu.VMEM((chunks, 2, series_rows, CHUNK), bf16),
            pltpu.VMEM((chunks, 2, series_rows, CHUNK), bf16),
            pltpu.VMEM((chunks, series_rows, CHUNK), bf16),
            pltpu.VMEM((chunks, series_rows, CHUNK), bf16),
            pltpu.SemaphoreType.DMA,
            sems(chunks),
            sems(2 * 3),
            sems(2 * n_tensor),
            sems(2 * n_tensor),
            sems(2 * n_tensor),
            sems(n_tensor - 1),
            sems(n_tensor - 1),
            sems(n_tensor - 1),
            sems(n_tensor - 1),
            sems(n_dp - 1),
            sems(n_dp - 1),
            sems(2 * chunks),
            sems(chunks),
        ],
        compiler_params=pltpu.CompilerParams(
            collective_id=0, has_side_effects=True, vmem_limit_bytes=60 * 1024 * 1024
        ),
    )(
        live_token_count,
        series_domain,
        output_gradient,
        attention_output,
        frozen_projection,
        domain_down_map,
        domain_up_map,
        common_down_map,
        common_up_map,
    )
    strip = width // 4

    def strips(*lead):
        shape = (*lead, strip)
        return pl.BlockSpec(shape, lambda i: (0,) * len(lead) + (i,))

    return pl.pallas_call(
        widen_kernel,
        grid=(width // strip,),
        out_shape=(
            jax.ShapeDtypeStruct((series_rows, width), bf16),
            jax.ShapeDtypeStruct((domains, rank, width), f32),
            jax.ShapeDtypeStruct((domains, rank, width), f32),
            jax.ShapeDtypeStruct((srank, width), f32),
            jax.ShapeDtypeStruct((srank, width), f32),
        ),
        in_specs=[strips(series_rows), strips(2 * side)],
        out_specs=(
            strips(series_rows),
            strips(domains, rank),
            strips(domains, rank),
            strips(srank),
            strips(srank),
        ),
        compiler_params=pltpu.CompilerParams(vmem_limit_bytes=32 * 1024 * 1024),
    )(grad_input, adapters)


def solution(mesh):
    placed = (
        P(("dp", "tensor"), None),
        P("dp", "tensor"),
        P("tensor", "dp"),
        P(None, None, "tensor"),
        P(None, None, "tensor"),
        P(None, "tensor"),
        P(None, "tensor"),
        P("dp"),
        P(),
    )
    n_dp, n_tensor = mesh.shape["dp"], mesh.shape["tensor"]
    on_one = on_device
    if n_dp == 2**3 and n_tensor == 2**2:
        on_one = functools.partial(on_cube, n_dp, n_tensor)
    return jax.shard_map(
        on_one,
        mesh=mesh,
        in_specs=placed,
        out_specs=(
            P("dp", "tensor"),
            P(None, None, "tensor"),
            P(None, None, "tensor"),
            P(None, "tensor"),
            P(None, "tensor"),
        ),
        check_vma=False,
    )
```

```python
import functools

import jax
import jax.numpy as jnp
from jax import lax
from jax.experimental import pallas as pl
from jax.experimental.pallas import tpu as pltpu
from jax.sharding import PartitionSpec as P

adapter_scale = 2.0
shared_scale = 2.0
contract_dims = (((1,), (1,)), ((), ()))
outer_dims = (((0,), (0,)), ((), ()))


def on_device(
    output_gradient,
    attention_output,
    frozen_projection,
    domain_down_map,
    domain_up_map,
    common_down_map,
    common_up_map,
    live_token_count,
    series_domain,
):
    rows_local = output_gradient.shape[0]
    tensor_index = lax.axis_index("tensor")
    rank_index = lax.axis_index("dp")
    domain_number = lax.dynamic_index_in_dim(series_domain, rank_index, 0, keepdims=False)
    local_down_map = lax.dynamic_index_in_dim(domain_down_map, domain_number, 0, keepdims=False)
    local_up_map = lax.dynamic_index_in_dim(domain_up_map, domain_number, 0, keepdims=False)
    positions = tensor_index * rows_local + lax.iota(jnp.int32, rows_local)
    live_rows = (positions < live_token_count[0])[:, None]
    masked = jnp.where(live_rows, output_gradient, jnp.zeros_like(output_gradient))
    down_part = lax.dot_general(
        attention_output, local_down_map, contract_dims, preferred_element_type=jnp.float32
    )
    shared_part = lax.dot_general(
        attention_output, common_down_map, contract_dims, preferred_element_type=jnp.float32
    )
    down_total, shared_total = lax.psum((down_part, shared_part), "tensor")
    reduced_activation = down_total.astype(jnp.bfloat16)
    low_shared = shared_total.astype(jnp.bfloat16)
    gathered = lax.all_gather(masked, "tensor", axis=0, tiled=True)
    column_width = local_up_map.shape[1]
    my_columns = lax.dynamic_slice_in_dim(gathered, tensor_index * column_width, column_width, 1)
    dom_partial = lax.dot_general(
        my_columns, local_up_map, contract_dims, preferred_element_type=jnp.float32
    )
    shared_partial = lax.dot_general(
        my_columns, common_up_map, contract_dims, preferred_element_type=jnp.float32
    )
    dom_total, shared_back_total = lax.psum((dom_partial, shared_partial), "tensor")
    domain_backward = dom_total.astype(jnp.bfloat16)
    back_shared = shared_back_total.astype(jnp.bfloat16)
    local_down_gradient = adapter_scale * lax.dot_general(
        domain_backward, attention_output, outer_dims, preferred_element_type=jnp.float32
    )
    local_up_gradient = adapter_scale * lax.dot_general(
        reduced_activation, my_columns, outer_dims, preferred_element_type=jnp.float32
    )
    grad_sdown = shared_scale * lax.dot_general(
        back_shared, attention_output, outer_dims, preferred_element_type=jnp.float32
    )
    grad_sup = shared_scale * lax.dot_general(
        low_shared, my_columns, outer_dims, preferred_element_type=jnp.float32
    )
    domain_picker = (lax.iota(jnp.int32, domain_down_map.shape[0]) == domain_number).astype(
        jnp.float32
    )[:, None, None]
    frozen_total = lax.dot_general(
        gathered,
        lax.all_gather(frozen_projection, "dp", axis=1, tiled=True),
        contract_dims,
        preferred_element_type=jnp.float32,
    )
    summed = lax.psum(
        (
            domain_picker * local_down_gradient[None],
            domain_picker * local_up_gradient[None],
            grad_sdown,
            grad_sup,
        ),
        "dp",
    )
    adapter_contribution = adapter_scale * jnp.dot(
        domain_backward, local_down_map, preferred_element_type=jnp.float32
    )
    adapter_contribution = adapter_contribution + shared_scale * jnp.dot(
        back_shared, common_down_map, preferred_element_type=jnp.float32
    )
    grad_input = (frozen_total + adapter_contribution).astype(jnp.bfloat16)
    return (grad_input, summed[0], summed[1], summed[2], summed[3])

MESH = pl.DeviceIdType.MESH
CHUNK = 256
AHEAD = 3
LATER = 2


def nt_dot(left, right):
    return lax.dot_general(left, right, contract_dims, preferred_element_type=jnp.float32)


def cube_kernel(
    dims,
    live_ref,
    domain_ref,
    grad_ref,
    act_ref,
    proj_ref,
    dom_down_ref,
    dom_up_ref,
    com_down_ref,
    com_up_ref,
    out_ref,
    adapters_ref,
    proj_mine,
    proj_other,
    masked_blocks,
    rows_all,
    up_all,
    down_map,
    low_send,
    low_recv,
    back_all,
    upg_send,
    upg_recv,
    sum_send,
    sum_recv,
    total_all,
    zl_send,
    zl_recv,
    zh_send,
    zh_recv,
    mine_sem,
    proj_sems,
    rowz_sems,
    rowx_sems,
    rowc_sems,
    rowf_sems,
    up_sems,
    low_sems,
    back_sems,
    upg_sems,
    sum_sems,
    total_sems,
    zl_sems,
    zh_sems,
):
    n_dp, n_tensor, chunks = dims
    dp = lax.axis_index("dp")
    tensor = lax.axis_index("tensor")
    y = lax.rem(dp, 2)
    z = dp // 2
    rows, block = masked_blocks.shape[1], masked_blocks.shape[2]
    series_rows = rows * n_tensor
    rank, srank = dom_down_ref.shape[1], com_down_ref.shape[0]
    ranks = rank + srank
    domains = dom_down_ref.shape[0]
    width = act_ref.shape[1]
    per_tensor = width // block
    piece = width // n_dp

    def flip(index, bit):
        return index + bit - 2 * bit * lax.rem(index // bit, 2)

    def flips(index, mask):
        for bit in (1, 2, 4):
            if mask & bit:
                index = flip(index, bit)
        return index

    def copy(src, dst, sems, at, dp_to, tensor_to):
        return pltpu.make_async_remote_copy(
            src_ref=src,
            dst_ref=dst,
            send_sem=sems.at[0, at],
            recv_sem=sems.at[1, at],
            device_id=(dp_to, tensor_to),
            device_id_type=MESH,
        )

    barrier = pltpu.get_barrier_semaphore()
    for mask in range(1, n_dp):
        pl.semaphore_signal(barrier, inc=1, device_id=(flips(dp, mask), tensor), device_id_type=MESH)
    for mask in range(1, n_tensor):
        pl.semaphore_signal(barrier, inc=1, device_id=(dp, flips(tensor, mask)), device_id_type=MESH)
    pl.semaphore_wait(barrier, n_dp + n_tensor - 2)

    def proj_copy(c):
        at = pl.ds(pl.multiple_of(c * CHUNK, CHUNK), CHUNK)
        return copy(proj_ref.at[at], proj_other.at[at], proj_sems, c, flip(dp, 1), tensor)

    def row_z(m, h):
        zt = flips(z, m)
        return copy(
            masked_blocks.at[zt * 2 + h],
            rows_all.at[m, tensor, h],
            rowz_sems,
            2 * (m - 1) + h,
            zt * 2 + y,
            tensor,
        )

    def row_x(m, h):
        here = rows_all.at[m, tensor, h]
        return copy(here, here, rowx_sems, 2 * m + h, dp, flip(tensor, 2))

    def row_core(m, h):
        here = rows_all.at[m, tensor, h]
        return copy(here, here, rowc_sems, 2 * m + h, dp, flip(tensor, 1))

    def row_forward(m, h):
        here = rows_all.at[m, flip(tensor, 2), h]
        return copy(here, here, rowf_sems, 2 * m + h, dp, flip(tensor, 1))

    def share_rows(m):
        for h in range(2):
            row_x(m, h).start()
            row_core(m, h).start()

    def up_copy(m):
        here = up_all.at[tensor]
        return copy(here, here, up_sems, m - 1, dp, flips(tensor, m))

    def low_copy(m):
        to = flips(tensor, m)
        return copy(low_send.at[to], low_recv.at[m - 1], low_sems, m - 1, dp, to)

    def back_copy(m):
        here = back_all.at[tensor]
        return copy(here, here, back_sems, m - 1, dp, flips(tensor, m))

    def upg_copy(m):
        to = flips(tensor, m)
        return copy(upg_send.at[to], upg_recv.at[m - 1], upg_sems, m - 1, dp, to)

    def sum_copy(m):
        to = flips(dp, m)
        return copy(sum_send.at[to], sum_recv.at[dp], sum_sems, m - 1, to, tensor)

    def total_copy(held, bit):
        here = total_all.at[flips(dp, held)]
        return copy(here, here, total_sems, (held | bit) - 1, flip(dp, bit), tensor)

    def zl_copy(k, c):
        part_of = zl_send.at[c, k]
        return copy(part_of, zl_recv.at[c, k], zl_sems, 2 * c + k, flip(z, 1) * 2 + y, tensor)

    def zh_copy(c):
        return copy(zh_send.at[c], zh_recv.at[c], zh_sems, c, flip(z, 2) * 2 + y, tensor)

    def partial(m, c):
        at = pl.ds(pl.multiple_of(c * CHUNK, CHUNK), CHUNK)
        own = rows_all[m, :, y].reshape(series_rows, block)
        other = rows_all[m, :, 1 - y].reshape(series_rows, block)
        return nt_dot(own, proj_mine[at, :]) + nt_dot(other, proj_other[at, :])

    def take_proj(c):
        proj_copy(c).wait_recv()

        proj_copy(c).wait_send()

        @pl.when(c + AHEAD < chunks)
        def _():
            proj_copy(c + AHEAD).start()

    def send_partial(k, c):
        zl_send[c, k] = partial(2 * k + 1, c).astype(jnp.bfloat16)
        zl_copy(k, c).start()

    def finish_rows(m):
        for h in range(2):
            row_x(m, h).wait_recv()
            row_forward(m, h).start()
        for h in range(2):
            row_core(m, h).wait_recv()
            row_forward(m, h).wait_recv()

    proj_copy(0).start()
    mine = pltpu.make_async_copy(proj_ref, proj_mine, mine_sem)
    mine.start()

    live = live_ref[0]
    alive = tensor * rows + lax.broadcasted_iota(jnp.int32, (rows, block), 0) < live
    for j in range(masked_blocks.shape[0]):
        part = grad_ref[:, j * block : (j + 1) * block]
        masked_blocks[j] = jnp.where(alive, part, jnp.zeros_like(part))
    row_z(1, 0).start()
    for h in range(2):
        rows_all[0, tensor, h] = masked_blocks[z * 2 + h]

    domain = domain_ref[dp]
    up_all[tensor, :rank] = dom_up_ref[domain]
    up_all[tensor, rank:] = com_up_ref[...]
    for m in range(1, n_tensor):
        up_copy(m).start()
    down_map[:rank] = dom_down_ref[domain]
    down_map[rank:] = com_down_ref[...]
    low_send[...] = jnp.zeros_like(low_send)
    back_all[tensor] = jnp.zeros_like(back_all.at[0])
    for j in range(n_tensor):
        low_send[j, :, :ranks] = nt_dot(act_ref[j * rows : (j + 1) * rows, :], down_map[...])
    for m in range(1, n_tensor):
        low_copy(m).start()

    row_z(1, 0).wait_send()
    row_z(1, 1).start()
    row_z(1, 0).wait_recv()
    row_x(1, 0).start()
    row_core(1, 0).start()
    row_z(1, 1).wait_send()
    for h in range(2):
        row_z(3, h).start()
    row_z(1, 1).wait_recv()
    row_x(1, 1).start()
    row_core(1, 1).start()
    proj_copy(1).start()
    finish_rows(1)
    share_rows(0)
    for c in range(2, AHEAD):
        proj_copy(c).start()

    mine.wait()
    take_proj(0)
    send_partial(0, 0)
    take_proj(1)
    send_partial(0, 1)
    for h in range(2):
        row_z(3, h).wait_send()
    for h in range(2):
        row_z(2, h).start()

    for h in range(2):
        row_z(3, h).wait_recv()
    share_rows(3)

    for m in range(1, n_tensor):
        up_copy(m).wait_recv()
    back = jnp.zeros((rows, ranks), jnp.float32)
    for j in range(masked_blocks.shape[0]):
        at = (j % per_tensor) * block
        back += nt_dot(masked_blocks[j], up_all[j // per_tensor, :, at : at + block])
    back_all[tensor, :, :ranks] = back.astype(jnp.bfloat16)
    for m in range(1, n_tensor):
        back_copy(m).start()

    low = low_send[tensor]
    for m in range(1, n_tensor):
        low_copy(m).wait_recv()
        low += low_recv[m - 1]
    low_flip = low.astype(jnp.bfloat16).astype(jnp.float32).T.astype(jnp.bfloat16)
    for j in range(masked_blocks.shape[0]):
        at = (j % per_tensor) * block
        part = adapter_scale * jnp.dot(
            low_flip, masked_blocks[j], preferred_element_type=jnp.float32
        )
        upg_send[j // per_tensor, :, at : at + block] = part[:ranks].astype(jnp.bfloat16)

    for m in range(1, n_tensor):
        upg_copy(m).start()
    finish_rows(3)
    send_partial(1, 0)
    send_partial(1, 1)
    take_proj(2)
    send_partial(0, 2)
    send_partial(1, 2)
    for h in range(2):
        row_z(2, h).wait_recv()
    share_rows(2)
    take_proj(3)
    send_partial(0, 3)
    send_partial(1, 3)
    finish_rows(2)
    finish_rows(0)
    early = 4

    lanes = back_all.shape[2]

    def send_sums():
        for m in range(1, n_tensor):
            back_copy(m).wait_recv()
        back_rows = back_all[...].reshape(series_rows, lanes)
        back_flip = back_rows.astype(jnp.float32).T.astype(jnp.bfloat16)
        for j in range(n_dp):
            at = slice(j * piece, (j + 1) * piece)
            part = adapter_scale * jnp.dot(
                back_flip, act_ref[:, at], preferred_element_type=jnp.float32
            )
            sum_send[j, :ranks] = part[:ranks].astype(jnp.bfloat16)
        for m in range(1, n_tensor):
            upg_copy(m).wait_recv()
        for j in range(n_dp):
            at = slice(j * piece, (j + 1) * piece)
            part = upg_send[tensor, :, at].astype(jnp.float32)
            for m in range(1, n_tensor):
                part += upg_recv[m - 1, :, at].astype(jnp.float32)
            sum_send[j, ranks:] = part.astype(jnp.bfloat16)
        for m in range(1, n_dp):
            sum_copy(m).start()
        sum_recv[dp] = sum_send[dp]

    def add_totals():
        for m in range(1, n_dp):
            sum_copy(m).wait_recv()
        for kind in range(2):
            base = kind * ranks
            to = kind * (domains * rank + srank)
            shared = jnp.zeros((srank, piece), jnp.float32)
            for r in range(n_dp):
                shared += sum_recv[r, base + rank : base + ranks].astype(jnp.float32)
            for k in range(domains):
                total = jnp.zeros((rank, piece), jnp.float32)
                for r in range(n_dp):
                    term = sum_recv[r, base : base + rank].astype(jnp.float32)
                    total += jnp.where(domain_ref[r] == k, term, jnp.zeros_like(term))
                total_all[dp, to + k * rank : to + (k + 1) * rank] = total.astype(jnp.bfloat16)
            to += domains * rank
            total_all[dp, to : to + srank] = shared.astype(jnp.bfloat16)

    def write_totals():
        for p in range(n_dp):
            adapters_ref[:, p * piece : (p + 1) * piece] = total_all[p]

    @pl.loop(0, chunks + 2)
    def _(c):
        @pl.when(c < chunks)
        def _():
            own = partial(2, c)
            zl_copy(1, c).wait_recv()
            zh_send[c] = (own + zl_recv[c, 1].astype(jnp.float32)).astype(jnp.bfloat16)
            zh_copy(c).start()

        @pl.when(c + early < chunks)
        def _():
            take_proj(c + early)
            send_partial(1, c + early)

        @pl.when(jnp.logical_and(c + LATER >= early, c + LATER < chunks))
        def _():
            send_partial(0, c + LATER)

        @pl.when(c >= 2)
        def _():
            a = c - 2
            at = pl.ds(pl.multiple_of(a * CHUNK, CHUNK), CHUNK)
            adapter = jnp.dot(
                back_all[...].reshape(series_rows, lanes)[:, :ranks],
                down_map[:, at],
                preferred_element_type=jnp.float32,
            )
            whole = partial(0, a) + adapter_scale * adapter
            zl_copy(0, a).wait_recv()
            zh_copy(a).wait_recv()
            whole += zl_recv[a, 0].astype(jnp.float32)
            out_ref[:, at] = (whole + zh_recv[a].astype(jnp.float32)).astype(jnp.bfloat16)

        @pl.when(c == 0)
        def _():
            send_sums()

        @pl.when(c == 4)
        def _():
            add_totals()
            total_copy(0, 4).start()

        @pl.when(c == 6)
        def _():
            total_copy(0, 4).wait_recv()
            for held in (0, 4):
                total_copy(held, 2).start()

        @pl.when(c == 7)
        def _():
            for held in (0, 4):
                total_copy(held, 2).wait_recv()
            for held in (0, 2, 4, 6):
                total_copy(held, 1).start()

        @pl.when(c == chunks + 1)
        def _():
            for held in (0, 2, 4, 6):
                total_copy(held, 1).wait_recv()
            write_totals()

    @pl.loop(0, chunks)
    def _(c):
        zl_copy(0, c).wait_send()
        zl_copy(1, c).wait_send()
        zh_copy(c).wait_send()

    for h in range(2):
        row_z(2, h).wait_send()
        for m in range(n_tensor):
            row_x(m, h).wait_send()
            row_core(m, h).wait_send()
            row_forward(m, h).wait_send()
    for m in range(1, n_tensor):
        up_copy(m).wait_send()
        low_copy(m).wait_send()
        back_copy(m).wait_send()
        upg_copy(m).wait_send()
    for m in range(1, n_dp):
        sum_copy(m).wait_send()
    for bit, helds in ((4, (0,)), (2, (0, 4)), (1, (0, 2, 4, 6))):
        for held in helds:
            total_copy(held, bit).wait_send()


def widen_kernel(grad_ref, sums_ref, grad_out, down_out, up_out, sdown_out, sup_out):
    grad_out[...] = grad_ref[...]
    domains, rank = down_out.shape[:2]
    first = 0
    for dom_out, com_out in ((down_out, sdown_out), (up_out, sup_out)):
        for k in range(domains):
            dom_out[k] = sums_ref[first : first + rank].astype(jnp.float32)
            first += rank
        com_out[...] = sums_ref[first : first + com_out.shape[0]].astype(jnp.float32)
        first += com_out.shape[0]


def on_cube(
    n_dp,
    n_tensor,
    output_gradient,
    attention_output,
    frozen_projection,
    domain_down_map,
    domain_up_map,
    common_down_map,
    common_up_map,
    live_token_count,
    series_domain,
):
    rows, model = output_gradient.shape
    series_rows, width = attention_output.shape
    block = frozen_projection.shape[1]
    domains, rank = domain_down_map.shape[:2]
    srank = common_down_map.shape[0]
    ranks, side = rank + srank, domains * rank + srank
    chunks, piece, blocks = width // CHUNK, width // n_dp, model // block
    lanes = 128
    bf16, f32 = jnp.bfloat16, jnp.float32
    vmem = pl.BlockSpec(memory_space=pltpu.VMEM)
    smem = pl.BlockSpec(memory_space=pltpu.SMEM)

    def sems(count):
        return pltpu.SemaphoreType.DMA((2, count))

    grad_input, adapters = pl.pallas_call(
        functools.partial(cube_kernel, (n_dp, n_tensor, chunks)),
        out_shape=(
            jax.ShapeDtypeStruct((series_rows, width), bf16),
            jax.ShapeDtypeStruct((2 * side, width), bf16),
        ),
        in_specs=[smem] * 2 + [vmem] * 2 + [pl.BlockSpec(memory_space=pl.ANY)] + [vmem] * 4,
        out_specs=(vmem,) * 2,
        scratch_shapes=[
            pltpu.VMEM((width, block), bf16),
            pltpu.VMEM((width, block), bf16),
            pltpu.VMEM((blocks, rows, block), bf16),
            pltpu.VMEM((4, n_tensor, 2, rows, block), bf16),
            pltpu.VMEM((n_tensor, ranks, width), bf16),
            pltpu.VMEM((ranks, width), bf16),
            pltpu.VMEM((n_tensor, rows, lanes), f32),
            pltpu.VMEM((n_tensor - 1, rows, lanes), f32),
            pltpu.VMEM((n_tensor, rows, lanes), bf16),
            pltpu.VMEM((n_tensor, ranks, width), bf16),
            pltpu.VMEM((n_tensor - 1, ranks, width), bf16),
            pltpu.VMEM((n_dp, 2 * ranks, piece), bf16),
            pltpu.VMEM((n_dp, 2 * ranks, piece), bf16),
            pltpu.VMEM((n_dp, 2 * side, piece), bf16),
            pltpu.VMEM((chunks, 2, series_rows, CHUNK), bf16),
            pltpu.VMEM((chunks, 2, series_rows, CHUNK), bf16),
            pltpu.VMEM((chunks, series_rows, CHUNK), bf16),
            pltpu.VMEM((chunks, series_rows, CHUNK), bf16),
            pltpu.SemaphoreType.DMA,
            sems(chunks),
            sems(2 * 3),
            sems(2 * n_tensor),
            sems(2 * n_tensor),
            sems(2 * n_tensor),
            sems(n_tensor - 1),
            sems(n_tensor - 1),
            sems(n_tensor - 1),
            sems(n_tensor - 1),
            sems(n_dp - 1),
            sems(n_dp - 1),
            sems(2 * chunks),
            sems(chunks),
        ],
        compiler_params=pltpu.CompilerParams(
            collective_id=0, has_side_effects=True, vmem_limit_bytes=60 * 1024 * 1024
        ),
    )(
        live_token_count,
        series_domain,
        output_gradient,
        attention_output,
        frozen_projection,
        domain_down_map,
        domain_up_map,
        common_down_map,
        common_up_map,
    )
    strip = width // 4

    def strips(*lead):
        shape = (*lead, strip)
        return pl.BlockSpec(shape, lambda i: (0,) * len(lead) + (i,))

    return pl.pallas_call(
        widen_kernel,
        grid=(width // strip,),
        out_shape=(
            jax.ShapeDtypeStruct((series_rows, width), bf16),
            jax.ShapeDtypeStruct((domains, rank, width), f32),
            jax.ShapeDtypeStruct((domains, rank, width), f32),
            jax.ShapeDtypeStruct((srank, width), f32),
            jax.ShapeDtypeStruct((srank, width), f32),
        ),
        in_specs=[strips(series_rows), strips(2 * side)],
        out_specs=(
            strips(series_rows),
            strips(domains, rank),
            strips(domains, rank),
            strips(srank),
            strips(srank),
        ),
        compiler_params=pltpu.CompilerParams(vmem_limit_bytes=60 * 1024 * 1024),
    )(grad_input, adapters)


def solution(mesh):
    placed = (
        P(("dp", "tensor"), None),
        P("dp", "tensor"),
        P("tensor", "dp"),
        P(None, None, "tensor"),
        P(None, None, "tensor"),
        P(None, "tensor"),
        P(None, "tensor"),
        P("dp"),
        P(),
    )
    n_dp, n_tensor = mesh.shape["dp"], mesh.shape["tensor"]
    on_one = on_device
    if n_dp == 2**3 and n_tensor == 2**2:
        on_one = functools.partial(on_cube, n_dp, n_tensor)
    return jax.shard_map(
        on_one,
        mesh=mesh,
        in_specs=placed,
        out_specs=(
            P("dp", "tensor"),
            P(None, None, "tensor"),
            P(None, None, "tensor"),
            P(None, "tensor"),
            P(None, "tensor"),
        ),
        check_vma=False,
    )
```

```python
import functools

import jax
import jax.numpy as jnp
from jax import lax
from jax.experimental import pallas as pl
from jax.experimental.pallas import tpu as pltpu
from jax.sharding import PartitionSpec as P

adapter_scale = 2.0
shared_scale = 2.0
contract_dims = (((1,), (1,)), ((), ()))
outer_dims = (((0,), (0,)), ((), ()))


def on_device(
    output_gradient,
    attention_output,
    frozen_projection,
    domain_down_map,
    domain_up_map,
    common_down_map,
    common_up_map,
    live_token_count,
    series_domain,
):
    rows_local = output_gradient.shape[0]
    tensor_index = lax.axis_index("tensor")
    rank_index = lax.axis_index("dp")
    domain_number = lax.dynamic_index_in_dim(series_domain, rank_index, 0, keepdims=False)
    local_down_map = lax.dynamic_index_in_dim(domain_down_map, domain_number, 0, keepdims=False)
    local_up_map = lax.dynamic_index_in_dim(domain_up_map, domain_number, 0, keepdims=False)
    positions = tensor_index * rows_local + lax.iota(jnp.int32, rows_local)
    live_rows = (positions < live_token_count[0])[:, None]
    masked = jnp.where(live_rows, output_gradient, jnp.zeros_like(output_gradient))
    down_part = lax.dot_general(
        attention_output, local_down_map, contract_dims, preferred_element_type=jnp.float32
    )
    shared_part = lax.dot_general(
        attention_output, common_down_map, contract_dims, preferred_element_type=jnp.float32
    )
    down_total, shared_total = lax.psum((down_part, shared_part), "tensor")
    reduced_activation = down_total.astype(jnp.bfloat16)
    low_shared = shared_total.astype(jnp.bfloat16)
    gathered = lax.all_gather(masked, "tensor", axis=0, tiled=True)
    column_width = local_up_map.shape[1]
    my_columns = lax.dynamic_slice_in_dim(gathered, tensor_index * column_width, column_width, 1)
    dom_partial = lax.dot_general(
        my_columns, local_up_map, contract_dims, preferred_element_type=jnp.float32
    )
    shared_partial = lax.dot_general(
        my_columns, common_up_map, contract_dims, preferred_element_type=jnp.float32
    )
    dom_total, shared_back_total = lax.psum((dom_partial, shared_partial), "tensor")
    domain_backward = dom_total.astype(jnp.bfloat16)
    back_shared = shared_back_total.astype(jnp.bfloat16)
    local_down_gradient = adapter_scale * lax.dot_general(
        domain_backward, attention_output, outer_dims, preferred_element_type=jnp.float32
    )
    local_up_gradient = adapter_scale * lax.dot_general(
        reduced_activation, my_columns, outer_dims, preferred_element_type=jnp.float32
    )
    grad_sdown = shared_scale * lax.dot_general(
        back_shared, attention_output, outer_dims, preferred_element_type=jnp.float32
    )
    grad_sup = shared_scale * lax.dot_general(
        low_shared, my_columns, outer_dims, preferred_element_type=jnp.float32
    )
    domain_picker = (lax.iota(jnp.int32, domain_down_map.shape[0]) == domain_number).astype(
        jnp.float32
    )[:, None, None]
    frozen_total = lax.dot_general(
        gathered,
        lax.all_gather(frozen_projection, "dp", axis=1, tiled=True),
        contract_dims,
        preferred_element_type=jnp.float32,
    )
    summed = lax.psum(
        (
            domain_picker * local_down_gradient[None],
            domain_picker * local_up_gradient[None],
            grad_sdown,
            grad_sup,
        ),
        "dp",
    )
    adapter_contribution = adapter_scale * jnp.dot(
        domain_backward, local_down_map, preferred_element_type=jnp.float32
    )
    adapter_contribution = adapter_contribution + shared_scale * jnp.dot(
        back_shared, common_down_map, preferred_element_type=jnp.float32
    )
    grad_input = (frozen_total + adapter_contribution).astype(jnp.bfloat16)
    return (grad_input, summed[0], summed[1], summed[2], summed[3])

MESH = pl.DeviceIdType.MESH
CHUNK = 256
AHEAD = 3


def nt_dot(left, right):
    return lax.dot_general(left, right, contract_dims, preferred_element_type=jnp.float32)


def cube_kernel(
    dims,
    live_ref,
    domain_ref,
    grad_ref,
    act_ref,
    proj_ref,
    dom_down_ref,
    dom_up_ref,
    com_down_ref,
    com_up_ref,
    out_ref,
    adapters_ref,
    proj_mine,
    proj_other,
    masked_blocks,
    rows_all,
    up_all,
    down_map,
    low_send,
    low_recv,
    back_all,
    upg_send,
    upg_recv,
    sum_send,
    sum_recv,
    total_all,
    zl_send,
    zl_recv,
    zh_send,
    zh_recv,
    mine_sem,
    proj_sems,
    rowz_sems,
    rowx_sems,
    rowc_sems,
    rowf_sems,
    up_sems,
    low_sems,
    back_sems,
    upg_sems,
    sum_sems,
    total_sems,
    zl_sems,
    zh_sems,
):
    n_dp, n_tensor, chunks = dims
    dp = lax.axis_index("dp")
    tensor = lax.axis_index("tensor")
    y = lax.rem(dp, 2)
    z = dp // 2
    rows, block = masked_blocks.shape[1], masked_blocks.shape[2]
    series_rows = rows * n_tensor
    rank, srank = dom_down_ref.shape[1], com_down_ref.shape[0]
    ranks = rank + srank
    domains = dom_down_ref.shape[0]
    width = act_ref.shape[1]
    per_tensor = width // block
    piece = width // n_dp

    def flip(index, bit):
        return index + bit - 2 * bit * lax.rem(index // bit, 2)

    def flips(index, mask):
        for bit in (1, 2, 4):
            if mask & bit:
                index = flip(index, bit)
        return index

    def copy(src, dst, sems, at, dp_to, tensor_to):
        return pltpu.make_async_remote_copy(
            src_ref=src,
            dst_ref=dst,
            send_sem=sems.at[0, at],
            recv_sem=sems.at[1, at],
            device_id=(dp_to, tensor_to),
            device_id_type=MESH,
        )

    barrier = pltpu.get_barrier_semaphore()
    for mask in range(1, n_dp):
        pl.semaphore_signal(barrier, inc=1, device_id=(flips(dp, mask), tensor), device_id_type=MESH)
    for mask in range(1, n_tensor):
        pl.semaphore_signal(barrier, inc=1, device_id=(dp, flips(tensor, mask)), device_id_type=MESH)
    pl.semaphore_wait(barrier, n_dp + n_tensor - 2)

    def proj_copy(c):
        at = pl.ds(pl.multiple_of(c * CHUNK, CHUNK), CHUNK)
        return copy(proj_ref.at[at], proj_other.at[at], proj_sems, c, flip(dp, 1), tensor)

    def row_z(m, h):
        zt = flips(z, m)
        return copy(
            masked_blocks.at[zt * 2 + h],
            rows_all.at[m, tensor, h],
            rowz_sems,
            2 * (m - 1) + h,
            zt * 2 + y,
            tensor,
        )

    def row_x(m, h):
        here = rows_all.at[m, tensor, h]
        return copy(here, here, rowx_sems, 2 * m + h, dp, flip(tensor, 2))

    def row_core(m, h):
        here = rows_all.at[m, tensor, h]
        return copy(here, here, rowc_sems, 2 * m + h, dp, flip(tensor, 1))

    def row_forward(m, h):
        here = rows_all.at[m, flip(tensor, 2), h]
        return copy(here, here, rowf_sems, 2 * m + h, dp, flip(tensor, 1))

    def share_half(m, h):
        row_x(m, h).start()
        row_core(m, h).start()

    def up_copy(m):
        here = up_all.at[tensor]
        return copy(here, here, up_sems, m - 1, dp, flips(tensor, m))

    def low_copy(m):
        to = flips(tensor, m)
        return copy(low_send.at[to], low_recv.at[m - 1], low_sems, m - 1, dp, to)

    def back_copy(m):
        here = back_all.at[tensor]
        return copy(here, here, back_sems, m - 1, dp, flips(tensor, m))

    def upg_copy(m):
        to = flips(tensor, m)
        return copy(upg_send.at[to], upg_recv.at[m - 1], upg_sems, m - 1, dp, to)

    def sum_copy(m):
        to = flips(dp, m)
        return copy(sum_send.at[to], sum_recv.at[dp], sum_sems, m - 1, to, tensor)

    def total_copy(held, bit):
        here = total_all.at[flips(dp, held)]
        return copy(here, here, total_sems, (held | bit) - 1, flip(dp, bit), tensor)

    def zl_copy(k, c):
        part_of = zl_send.at[c, k]
        return copy(part_of, zl_recv.at[c, k], zl_sems, 2 * c + k, flip(z, 1) * 2 + y, tensor)

    def zh_copy(c):
        return copy(zh_send.at[c], zh_recv.at[c], zh_sems, c, flip(z, 2) * 2 + y, tensor)

    def partial(m, c):
        at = pl.ds(pl.multiple_of(c * CHUNK, CHUNK), CHUNK)
        own = rows_all[m, :, y].reshape(series_rows, block)
        other = rows_all[m, :, 1 - y].reshape(series_rows, block)
        return nt_dot(own, proj_mine[at, :]) + nt_dot(other, proj_other[at, :])

    def take_proj(c):
        proj_copy(c).wait_recv()

        proj_copy(c).wait_send()

        @pl.when(c + AHEAD < chunks)
        def _():
            proj_copy(c + AHEAD).start()

    def send_partial(k, c):
        zl_send[c, k] = partial(2 * k + 1, c).astype(jnp.bfloat16)
        zl_copy(k, c).start()

    def finish_rows(m):
        for h in range(2):
            row_x(m, h).wait_recv()
            row_forward(m, h).start()
        for h in range(2):
            row_core(m, h).wait_recv()
            row_forward(m, h).wait_recv()

    proj_copy(0).start()
    mine = pltpu.make_async_copy(proj_ref, proj_mine, mine_sem)
    mine.start()

    live = live_ref[0]
    alive = tensor * rows + lax.broadcasted_iota(jnp.int32, (rows, block), 0) < live
    for j in range(masked_blocks.shape[0]):
        part = grad_ref[:, j * block : (j + 1) * block]
        masked_blocks[j] = jnp.where(alive, part, jnp.zeros_like(part))
    row_z(1, 0).start()
    for h in range(2):
        row_z(3, h).start()
    for h in range(2):
        rows_all[0, tensor, h] = masked_blocks[z * 2 + h]

    domain = domain_ref[dp]
    up_all[tensor, :rank] = dom_up_ref[domain]
    up_all[tensor, rank:] = com_up_ref[...]
    for m in range(1, n_tensor):
        up_copy(m).start()
    down_map[:rank] = dom_down_ref[domain]
    down_map[rank:] = com_down_ref[...]
    low_send[...] = jnp.zeros_like(low_send)
    back_all[tensor] = jnp.zeros_like(back_all.at[0])
    for j in range(n_tensor):
        low_send[j, :, :ranks] = nt_dot(act_ref[j * rows : (j + 1) * rows, :], down_map[...])
    for m in range(1, n_tensor):
        low_copy(m).start()

    row_z(1, 0).wait_send()
    row_z(1, 1).start()
    row_z(1, 0).wait_recv()
    row_x(1, 0).start()
    row_core(1, 0).start()
    row_z(1, 1).wait_send()
    row_z(1, 1).wait_recv()
    row_x(1, 1).start()
    row_core(1, 1).start()
    proj_copy(1).start()
    finish_rows(1)
    for c in range(2, AHEAD):
        proj_copy(c).start()

    for h in range(2):
        row_z(3, h).wait_send()
    for h in range(2):
        row_z(2, h).start()
    mine.wait()
    take_proj(0)
    send_partial(0, 0)
    take_proj(1)
    send_partial(0, 1)

    for h in range(2):
        row_z(3, h).wait_recv()
        share_half(3, h)

    for m in range(1, n_tensor):
        up_copy(m).wait_recv()
    back = jnp.zeros((rows, ranks), jnp.float32)
    for j in range(masked_blocks.shape[0]):
        at = (j % per_tensor) * block
        back += nt_dot(masked_blocks[j], up_all[j // per_tensor, :, at : at + block])
    back_all[tensor, :, :ranks] = back.astype(jnp.bfloat16)
    for m in range(1, n_tensor):
        back_copy(m).start()

    low = low_send[tensor]
    for m in range(1, n_tensor):
        low_copy(m).wait_recv()
        low += low_recv[m - 1]
    low_flip = low.astype(jnp.bfloat16).astype(jnp.float32).T.astype(jnp.bfloat16)
    for j in range(masked_blocks.shape[0]):
        at = (j % per_tensor) * block
        part = adapter_scale * jnp.dot(
            low_flip, masked_blocks[j], preferred_element_type=jnp.float32
        )
        upg_send[j // per_tensor, :, at : at + block] = part[:ranks].astype(jnp.bfloat16)

    for m in range(1, n_tensor):
        upg_copy(m).start()
    finish_rows(3)
    send_partial(1, 0)
    send_partial(1, 1)
    take_proj(2)
    send_partial(0, 2)
    send_partial(1, 2)
    for h in range(2):
        row_z(2, h).wait_recv()
        share_half(2, h)
    take_proj(3)
    send_partial(0, 3)
    send_partial(1, 3)
    finish_rows(2)
    for h in range(2):
        share_half(0, h)
    early = 4

    lanes = back_all.shape[2]

    def send_sums():
        for m in range(1, n_tensor):
            back_copy(m).wait_recv()
        back_rows = back_all[...].reshape(series_rows, lanes)
        back_flip = back_rows.astype(jnp.float32).T.astype(jnp.bfloat16)
        for j in range(n_dp):
            at = slice(j * piece, (j + 1) * piece)
            part = adapter_scale * jnp.dot(
                back_flip, act_ref[:, at], preferred_element_type=jnp.float32
            )
            sum_send[j, :ranks] = part[:ranks].astype(jnp.bfloat16)
        for m in range(1, n_tensor):
            upg_copy(m).wait_recv()
        for j in range(n_dp):
            at = slice(j * piece, (j + 1) * piece)
            part = upg_send[tensor, :, at].astype(jnp.float32)
            for m in range(1, n_tensor):
                part += upg_recv[m - 1, :, at].astype(jnp.float32)
            sum_send[j, ranks:] = part.astype(jnp.bfloat16)
        for m in range(1, n_dp):
            sum_copy(m).start()
        sum_recv[dp] = sum_send[dp]

    def add_totals():
        for m in range(1, n_dp):
            sum_copy(m).wait_recv()
        for kind in range(2):
            base = kind * ranks
            to = kind * (domains * rank + srank)
            shared = jnp.zeros((srank, piece), jnp.float32)
            for r in range(n_dp):
                shared += sum_recv[r, base + rank : base + ranks].astype(jnp.float32)
            for k in range(domains):
                total = jnp.zeros((rank, piece), jnp.float32)
                for r in range(n_dp):
                    term = sum_recv[r, base : base + rank].astype(jnp.float32)
                    total += jnp.where(domain_ref[r] == k, term, jnp.zeros_like(term))
                total_all[dp, to + k * rank : to + (k + 1) * rank] = total.astype(jnp.bfloat16)
            to += domains * rank
            total_all[dp, to : to + srank] = shared.astype(jnp.bfloat16)

    def write_totals():
        for p in range(n_dp):
            adapters_ref[:, p * piece : (p + 1) * piece] = total_all[p]

    @pl.loop(0, chunks + 2)
    def _(c):
        @pl.when(c < chunks)
        def _():
            own = partial(2, c)
            zl_copy(1, c).wait_recv()
            zh_send[c] = (own + zl_recv[c, 1].astype(jnp.float32)).astype(jnp.bfloat16)
            zh_copy(c).start()

        @pl.when(c + early < chunks)
        def _():
            take_proj(c + early)
            send_partial(0, c + early)
            send_partial(1, c + early)

        @pl.when(c >= 2)
        def _():
            a = c - 2
            at = pl.ds(pl.multiple_of(a * CHUNK, CHUNK), CHUNK)
            adapter = jnp.dot(
                back_all[...].reshape(series_rows, lanes)[:, :ranks],
                down_map[:, at],
                preferred_element_type=jnp.float32,
            )
            whole = partial(0, a) + adapter_scale * adapter
            zl_copy(0, a).wait_recv()
            zh_copy(a).wait_recv()
            whole += zl_recv[a, 0].astype(jnp.float32)
            out_ref[:, at] = (whole + zh_recv[a].astype(jnp.float32)).astype(jnp.bfloat16)

        @pl.when(c == 1)
        def _():
            finish_rows(0)
            send_sums()

        @pl.when(c == 3)
        def _():
            add_totals()
            total_copy(0, 4).start()

        @pl.when(c == 5)
        def _():
            total_copy(0, 4).wait_recv()
            for held in (0, 4):
                total_copy(held, 2).start()

        @pl.when(c == 6)
        def _():
            for held in (0, 4):
                total_copy(held, 2).wait_recv()
            for held in (0, 2, 4, 6):
                total_copy(held, 1).start()

        @pl.when(c == chunks)
        def _():
            for held in (0, 2, 4, 6):
                total_copy(held, 1).wait_recv()
            write_totals()

    @pl.loop(0, chunks)
    def _(c):
        zl_copy(0, c).wait_send()
        zl_copy(1, c).wait_send()
        zh_copy(c).wait_send()

    for h in range(2):
        row_z(2, h).wait_send()
        for m in range(n_tensor):
            row_x(m, h).wait_send()
            row_core(m, h).wait_send()
            row_forward(m, h).wait_send()
    for m in range(1, n_tensor):
        up_copy(m).wait_send()
        low_copy(m).wait_send()
        back_copy(m).wait_send()
        upg_copy(m).wait_send()
    for m in range(1, n_dp):
        sum_copy(m).wait_send()
    for bit, helds in ((4, (0,)), (2, (0, 4)), (1, (0, 2, 4, 6))):
        for held in helds:
            total_copy(held, bit).wait_send()


def widen_kernel(grad_ref, sums_ref, grad_out, down_out, up_out, sdown_out, sup_out):
    grad_out[...] = grad_ref[...]
    domains, rank = down_out.shape[:2]
    first = 0
    for dom_out, com_out in ((down_out, sdown_out), (up_out, sup_out)):
        for k in range(domains):
            dom_out[k] = sums_ref[first : first + rank].astype(jnp.float32)
            first += rank
        com_out[...] = sums_ref[first : first + com_out.shape[0]].astype(jnp.float32)
        first += com_out.shape[0]


def on_cube(
    n_dp,
    n_tensor,
    output_gradient,
    attention_output,
    frozen_projection,
    domain_down_map,
    domain_up_map,
    common_down_map,
    common_up_map,
    live_token_count,
    series_domain,
):
    rows, model = output_gradient.shape
    series_rows, width = attention_output.shape
    block = frozen_projection.shape[1]
    domains, rank = domain_down_map.shape[:2]
    srank = common_down_map.shape[0]
    ranks, side = rank + srank, domains * rank + srank
    chunks, piece, blocks = width // CHUNK, width // n_dp, model // block
    lanes = 128
    bf16, f32 = jnp.bfloat16, jnp.float32
    vmem = pl.BlockSpec(memory_space=pltpu.VMEM)
    smem = pl.BlockSpec(memory_space=pltpu.SMEM)

    def sems(count):
        return pltpu.SemaphoreType.DMA((2, count))

    grad_input, adapters = pl.pallas_call(
        functools.partial(cube_kernel, (n_dp, n_tensor, chunks)),
        out_shape=(
            jax.ShapeDtypeStruct((series_rows, width), bf16),
            jax.ShapeDtypeStruct((2 * side, width), bf16),
        ),
        in_specs=[smem] * 2 + [vmem] * 2 + [pl.BlockSpec(memory_space=pl.ANY)] + [vmem] * 4,
        out_specs=(vmem,) * 2,
        scratch_shapes=[
            pltpu.VMEM((width, block), bf16),
            pltpu.VMEM((width, block), bf16),
            pltpu.VMEM((blocks, rows, block), bf16),
            pltpu.VMEM((4, n_tensor, 2, rows, block), bf16),
            pltpu.VMEM((n_tensor, ranks, width), bf16),
            pltpu.VMEM((ranks, width), bf16),
            pltpu.VMEM((n_tensor, rows, lanes), f32),
            pltpu.VMEM((n_tensor - 1, rows, lanes), f32),
            pltpu.VMEM((n_tensor, rows, lanes), bf16),
            pltpu.VMEM((n_tensor, ranks, width), bf16),
            pltpu.VMEM((n_tensor - 1, ranks, width), bf16),
            pltpu.VMEM((n_dp, 2 * ranks, piece), bf16),
            pltpu.VMEM((n_dp, 2 * ranks, piece), bf16),
            pltpu.VMEM((n_dp, 2 * side, piece), bf16),
            pltpu.VMEM((chunks, 2, series_rows, CHUNK), bf16),
            pltpu.VMEM((chunks, 2, series_rows, CHUNK), bf16),
            pltpu.VMEM((chunks, series_rows, CHUNK), bf16),
            pltpu.VMEM((chunks, series_rows, CHUNK), bf16),
            pltpu.SemaphoreType.DMA,
            sems(chunks),
            sems(2 * 3),
            sems(2 * n_tensor),
            sems(2 * n_tensor),
            sems(2 * n_tensor),
            sems(n_tensor - 1),
            sems(n_tensor - 1),
            sems(n_tensor - 1),
            sems(n_tensor - 1),
            sems(n_dp - 1),
            sems(n_dp - 1),
            sems(2 * chunks),
            sems(chunks),
        ],
        compiler_params=pltpu.CompilerParams(
            collective_id=0, has_side_effects=True, vmem_limit_bytes=60 * 1024 * 1024
        ),
    )(
        live_token_count,
        series_domain,
        output_gradient,
        attention_output,
        frozen_projection,
        domain_down_map,
        domain_up_map,
        common_down_map,
        common_up_map,
    )
    strip = width // 4

    def strips(*lead):
        shape = (*lead, strip)
        return pl.BlockSpec(shape, lambda i: (0,) * len(lead) + (i,))

    return pl.pallas_call(
        widen_kernel,
        grid=(width // strip,),
        out_shape=(
            jax.ShapeDtypeStruct((series_rows, width), bf16),
            jax.ShapeDtypeStruct((domains, rank, width), f32),
            jax.ShapeDtypeStruct((domains, rank, width), f32),
            jax.ShapeDtypeStruct((srank, width), f32),
            jax.ShapeDtypeStruct((srank, width), f32),
        ),
        in_specs=[strips(series_rows), strips(2 * side)],
        out_specs=(
            strips(series_rows),
            strips(domains, rank),
            strips(domains, rank),
            strips(srank),
            strips(srank),
        ),
        compiler_params=pltpu.CompilerParams(vmem_limit_bytes=60 * 1024 * 1024),
    )(grad_input, adapters)


def solution(mesh):
    placed = (
        P(("dp", "tensor"), None),
        P("dp", "tensor"),
        P("tensor", "dp"),
        P(None, None, "tensor"),
        P(None, None, "tensor"),
        P(None, "tensor"),
        P(None, "tensor"),
        P("dp"),
        P(),
    )
    n_dp, n_tensor = mesh.shape["dp"], mesh.shape["tensor"]
    on_one = on_device
    if n_dp == 2**3 and n_tensor == 2**2:
        on_one = functools.partial(on_cube, n_dp, n_tensor)
    return jax.shard_map(
        on_one,
        mesh=mesh,
        in_specs=placed,
        out_specs=(
            P("dp", "tensor"),
            P(None, None, "tensor"),
            P(None, None, "tensor"),
            P(None, "tensor"),
            P(None, "tensor"),
        ),
        check_vma=False,
    )
```
